512 devices in a mesh: dp: 64 (over y, x, core), tensor: 8 (over z).
Axes of the slice: x: 4, y: 8, z: 8, core: 2. Of those that a mesh axis runs over, the one named last changes fastest.
Arguments:
- grad_terms: bfloat16 [8, 8192, 12288], P('tensor', 'dp'), may hold values from -24 to 24
- acts: bfloat16 [8192, 12288], P('dp', 'tensor'), may hold values from -24 to 24
- kept: int32 [64, 8, 32], P('dp', 'tensor'), may hold values from 0 to 1151, as said below
- starts: int32 [8, 64], P('tensor'), may hold values from 0 to 1148, as said below
Outputs:
- normed: bfloat16 [64, 8, 32, 128, 128], P('dp', 'tensor')
The draws below stay inside these ranges and needn't reach their ends.
Inputs may be any that keep to these rules, and one draw needn't show every extreme that they name: kept[r, t] lists distinct blocks of rank t's gradient, block b covering rows 128 * (b // 96) and columns 128 * (b % 96) of it. A replica keeps either no block or exactly 2 blocks of each owner's region. At most 4 distinct blocks of one region are kept by all replicas together. Every region holds a kept block, and some owner's region has 2 blocks kept by every replica. starts[t, 0] is 0; starts rise, and each region, from starts[t, o] up to the next start (or 1152), holds 4 or more blocks.
All inputs are finite; a program needn't handle non-finite values.
Results may differ from the reference program's by a relative error of at most 0.022.
Values may be sent and summed in bfloat16 or wider, within the bound.
A program may use at most 64 MiB of HBM per device.

```python
import math
import jax
import jax.numpy as jnp
from jax import lax

D = 12288
TOK_DEV = 128
BLOCK = 128
POOL = 4
NBR = 12
NBC = 96
NB = 1152
KEPT = 32
TOKENS = 8192
N_DP = 64
N_TENSOR = 8


def structure(key):

    def one_rank(rank_key):
        k_cut, k_pool, k_owner, k_rep, k_first, k_step, k_order = jax.random.split(rank_key, 7)
        spare_blocks = NB - N_DP * POOL
        cut_points = jnp.sort(jax.random.randint(k_cut, (N_DP - 1,), 0, spare_blocks + 1))
        starts_r = jnp.concatenate([jnp.zeros((1,), jnp.int32), cut_points.astype(jnp.int32) + POOL * jnp.arange(1, N_DP, dtype=jnp.int32)])
        region_ends = jnp.concatenate([starts_r[1:], jnp.full((1,), NB, jnp.int32)])
        stride = (region_ends - starts_r) // POOL
        jitter = jax.random.randint(k_pool, (N_DP, POOL), 0, 1 << 20) % stride[:, None]
        pool_blocks = starts_r[:, None] + jnp.arange(POOL, dtype=jnp.int32)[None, :] * stride[:, None] + jitter
        owners_each = N_DP // 4
        counts = jnp.concatenate([jnp.full((1,), N_DP, jnp.int32), jnp.full((N_DP - owners_each,), owners_each - 1, jnp.int32), jnp.full((owners_each - 1,), owners_each, jnp.int32)])
        ends_c = jnp.cumsum(counts)
        entries = jnp.arange(N_DP * owners_each, dtype=jnp.int32)
        rank_of = jnp.searchsorted(ends_c, entries, side='right').astype(jnp.int32)
        position = entries - (ends_c[rank_of] - counts[rank_of])
        owner_perm = jax.random.permutation(k_owner, N_DP)
        owner_of = owner_perm[rank_of]
        offset = jax.random.randint(k_first, (N_DP,), 0, POOL)
        first_pick = (position + offset[owner_of]) % POOL
        second = (first_pick + 1 + jax.random.randint(k_step, (N_DP * owners_each,), 0, POOL - 1)) % POOL
        blocks = jnp.stack([pool_blocks[owner_of, first_pick], pool_blocks[owner_of, second]], axis=1)
        kept_rows = blocks.reshape(owners_each, N_DP, 2).transpose(1, 0, 2).reshape(N_DP, 2 * owners_each)
        kept_rows = kept_rows[jax.random.permutation(k_rep, N_DP)]
        row_keys = jax.random.split(k_order, N_DP)
        kept_rows = jax.vmap(lambda row_key, row: jax.random.permutation(row_key, row))(row_keys, kept_rows)
        return (starts_r, kept_rows.astype(jnp.int32))
    rank_keys = jax.random.split(key, N_TENSOR)
    starts_all, kept_all = jax.vmap(one_rank)(rank_keys)
    return (starts_all.astype(jnp.int32), jnp.transpose(kept_all, (1, 0, 2)).astype(jnp.int32))


def scaled_field(key, shape, col_lo, col_hi):
    k_col = jax.random.fold_in(key, 0)
    k_row = jax.random.fold_in(key, 1)
    k_noise = jax.random.fold_in(key, 3)
    columns = jnp.exp(jax.random.uniform(k_col, (shape[-1],), jnp.float32, math.log(col_lo), math.log(col_hi)))
    row_scale = jnp.exp(jax.random.uniform(k_row, (shape[-2],), jnp.float32, math.log(0.5), math.log(2.0)))
    base = jnp.clip(jax.random.normal(k_noise, shape, jnp.float32), -4.0, 4.0)
    return base * row_scale[:, None] * columns


def draw_grad_terms(key, part):
    key = jax.random.fold_in(key, 11)
    return scaled_field(key, (N_TENSOR, TOKENS, D), 0.3, 3.0).astype(jnp.bfloat16)


def draw_acts(key, part):
    key = jax.random.fold_in(key, 23)
    return scaled_field(key, (TOKENS, D), 0.3, 3.0).astype(jnp.bfloat16)


def draw_kept(key, part):
    return structure(key)[1]


def draw_starts(key, part):
    return structure(key)[0]


def setup_inputs(seed: int = 0) -> dict:
    key_list = jax.random.split(jax.random.key(seed), 5)
    grad_terms = draw_grad_terms(jax.random.fold_in(key_list[4], 71), 0)
    acts = draw_acts(jax.random.fold_in(key_list[4], 71), 0)
    kept = draw_kept(jax.random.fold_in(key_list[4], 71), 0)
    starts = draw_starts(jax.random.fold_in(key_list[4], 71), 0)
    return {"grad_terms": grad_terms, "acts": acts, "kept": kept, "starts": starts}


epsilon = 1e-06

def reference(grad_terms, acts, kept, starts):
    gradient = jnp.zeros((TOKENS, D), jnp.float32)
    for tensor_rank in range(N_TENSOR):
        gradient = gradient + grad_terms[tensor_rank].astype(jnp.float32)
    gradient = gradient.astype(jnp.bfloat16)
    grad_cols = gradient.astype(jnp.float32).reshape(TOKENS, NBC, BLOCK)
    in_rows = D // N_TENSOR

    def per_rank(tensor_rank):
        acts_t = lax.dynamic_slice_in_dim(acts, tensor_rank * in_rows, in_rows, 1)
        acts_t = acts_t.astype(jnp.float32).reshape(TOKENS, NBR, BLOCK)
        kept_t = jnp.take(kept, tensor_rank, axis=1)
        starts_t = jnp.take(starts, tensor_rank, axis=0)

        def per_replica(replica):
            act_rows = lax.dynamic_slice_in_dim(acts_t, replica * TOK_DEV, TOK_DEV, 0)
            grad_rows = lax.dynamic_slice_in_dim(grad_cols, replica * TOK_DEV, TOK_DEV, 0)
            block_ids = jnp.take(kept_t, replica, axis=0)
            left_cols = jnp.take(act_rows, block_ids // NBC, axis=1)
            right_cols = jnp.take(grad_rows, block_ids % NBC, axis=1)
            return jnp.einsum('tkr,tkc->krc', left_cols, right_cols)
        products = lax.map(per_replica, jnp.arange(N_DP, dtype=jnp.int32))
        products = lax.optimization_barrier(products.astype(jnp.bfloat16)).astype(jnp.float32)
        flat_ids = kept_t.reshape(-1)
        dense_sums = jax.ops.segment_sum(products.reshape(N_DP * KEPT, BLOCK * BLOCK), flat_ids, num_segments=NB)
        marked = jax.ops.segment_sum(jnp.ones((N_DP * KEPT,), jnp.float32), flat_ids, num_segments=NB) > 0
        region = lax.optimization_barrier(jnp.sum((starts_t[None, :] <= jnp.arange(NB, dtype=jnp.int32)[:, None]).astype(jnp.int32), axis=1)) - 1
        energy = jax.ops.segment_sum(jnp.where(marked, lax.optimization_barrier(jnp.sum(dense_sums * dense_sums, axis=1)), 0.0), region, num_segments=N_DP)
        counted = jax.ops.segment_sum(marked.astype(jnp.float32), region, num_segments=N_DP)
        mean_sq = energy / (counted * (BLOCK * BLOCK))
        factor = lax.rsqrt(mean_sq + epsilon)
        picked = jnp.take(dense_sums, flat_ids, axis=0) * jnp.take(factor, jnp.take(region, flat_ids))[:, None]
        return picked.astype(jnp.bfloat16).reshape(N_DP, KEPT, BLOCK, BLOCK)
    normed = lax.map(per_rank, jnp.arange(N_TENSOR, dtype=jnp.int32))
    return jnp.transpose(normed, (1, 0, 2, 3, 4))
```

```python
import jax
import jax.numpy as jnp
from jax import lax
from jax.sharding import PartitionSpec as P

BLOCK = 128
POOL = 4


epsilon = 1e-06


def pool_places(kept, starts, blocks):
    owners = starts.shape[0]
    mine = kept[0]
    everyone = lax.all_gather(kept, "dp", axis=0, tiled=True).reshape(-1)
    ids = jnp.arange(blocks, dtype=jnp.int32)
    marked = jnp.any(everyone[:, None] == ids[None, :], axis=0)
    region = jnp.sum((starts[None, :] <= mine[:, None]).astype(jnp.int32), axis=1) - 1
    first = jnp.sum(
        jnp.where(region[:, None] == jnp.arange(owners)[None, :], starts[None, :], 0), axis=1
    )
    before = marked[None, :] & (ids[None, :] >= first[:, None]) & (ids[None, :] < mine[:, None])
    place = region * POOL + jnp.sum(before.astype(jnp.int32), axis=1)
    ends = jnp.concatenate([starts[1:], jnp.full((1,), blocks, jnp.int32)])
    inside = marked[None, :] & (ids[None, :] >= starts[:, None]) & (ids[None, :] < ends[:, None])
    count = jnp.sum(inside.astype(jnp.float32), axis=1)
    return place, count


def shards(grad_terms, acts, kept, starts):
    tok_rows = acts.shape[0]
    features = grad_terms.shape[2]
    col_blocks = features // BLOCK
    row_blocks = acts.shape[1] // BLOCK
    owners = lax.axis_size("dp")
    places = owners * POOL
    chosen = kept[0, 0]
    slots = chosen.shape[0]
    place, count = pool_places(kept[0], starts[0], row_blocks * col_blocks)
    summed = lax.psum(grad_terms[0], "tensor")
    sel_a = jnp.take(acts.reshape(tok_rows, row_blocks, BLOCK), chosen // col_blocks, axis=1)
    sel_g = jnp.take(summed.reshape(tok_rows, col_blocks, BLOCK), chosen % col_blocks, axis=1)
    tiles = jnp.einsum("tkr,tkc->krc", sel_a, sel_g, preferred_element_type=jnp.float32)
    tiles = tiles.astype(jnp.bfloat16)
    hit = place[None, :] == jnp.arange(places, dtype=jnp.int32)[:, None]
    source = jnp.sum(jnp.where(hit, jnp.arange(slots, dtype=jnp.int32)[None, :], 0), axis=1)
    filled = jnp.any(hit, axis=1)
    terms = jnp.where(filled[:, None, None], jnp.take(tiles, source, axis=0), jnp.zeros((), jnp.bfloat16))
    totals = lax.psum_scatter(terms, "dp", scatter_dimension=0, tiled=True).astype(jnp.float32)
    me = lax.axis_index("dp")
    energy = jnp.sum(totals * totals)
    mean_sq = energy / (lax.dynamic_index_in_dim(count, me, keepdims=False) * (BLOCK * BLOCK))
    normed = (totals * lax.rsqrt(mean_sq + epsilon)).astype(jnp.bfloat16)
    gathered = lax.all_gather(normed, "dp", axis=0, tiled=True)
    return jnp.take(gathered, place, axis=0)[None, None]


def solution(mesh):
    placed = (
        P("tensor", "dp", None),
        P("dp", "tensor"),
        P("dp", "tensor", None),
        P("tensor", None),
    )
    return jax.shard_map(
        shards,
        mesh=mesh,
        in_specs=placed,
        out_specs=P("dp", "tensor", None, None, None),
        check_vma=False,
    )
```

```python
import functools

import jax
import jax.numpy as jnp
from jax import lax
from jax.experimental import pallas as pl
from jax.experimental.pallas import tpu as pltpu
from jax.sharding import PartitionSpec as P

BLOCK = 128
POOL = 4
ROW = 8
SUBS = 4
BATCHES = 4

epsilon = 1e-06
MESH = pl.DeviceIdType.MESH
f32, bf16, i32 = jnp.float32, jnp.bfloat16, jnp.int32


def body(
    Y, R, Z, NB,
    grad, acts, kept, starts, out,
    own, zr, gsum, pack, gsel, acts_t, tiles, xr, ys, yr, tot, eb, fac, full, opack,
    mine, kz, kr, marks, tab, srcv,
    kz_s, kr_s, c_s, p_s, src_s,
    own_sem, kz_sem, kr_sem, mk_sem, loc_sem, zrs_sem, za_sem, xa_sem, yrs_sem, e_sem, yag_sem, ret_sem,
):
    dp, t = lax.axis_index("dp"), lax.axis_index("tensor")
    y, s = dp // R, lax.rem(dp, R)
    K = out.shape[0]
    D = own.shape[1]
    rz, rr = BLOCK // Z, BLOCK // R
    cols = D // BLOCK
    SL = POOL * R
    KB = K // BATCHES
    owners = Y * R
    pending = []

    def z_dev(d):
        return (dp, lax.rem(t + d + Z, Z))

    def row_dev(d):
        return (y * R + lax.rem(s + d + R, R), t)

    def y_dev(d):
        return (lax.rem(y + d + Y, Y) * R + s, t)

    def send(src, dst, sems, index, device):
        copy = pltpu.make_async_remote_copy(
            src_ref=src, dst_ref=dst,
            send_sem=sems.at[(0,) + index], recv_sem=sems.at[(1,) + index],
            device_id=device, device_id_type=MESH,
        )
        copy.start()
        pending.append(copy)

    def arrived(dst, sems, index, device):
        pltpu.make_async_remote_copy(
            src_ref=dst, dst_ref=dst,
            send_sem=sems.at[(0,) + index], recv_sem=sems.at[(1,) + index],
            device_id=device, device_id_type=MESH,
        ).wait_recv()

    barrier = pltpu.get_barrier_semaphore()
    partners = [z_dev(d) for d in range(1, Z)] + [row_dev(d) for d in range(1, R)]
    partners += [y_dev(1)] + ([y_dev(-1)] if Y > 2 else [])
    for device in partners:
        pl.semaphore_signal(barrier, inc=1, device_id=device, device_id_type=MESH)
    mine[...] = jnp.full(mine.shape, -1, i32)
    mine[0:1, 0:K] = kept[...]
    for i in range(Z):
        rows = pl.ds(pl.multiple_of(i * rz, rz), rz)
        pltpu.make_async_copy(grad.at[0, rows, :], own.at[rows, :], own_sem.at[i]).start()
    pl.semaphore_wait(barrier, len(partners))

    for d in range(1, Z):
        send(mine, kz.at[d], kz_sem, (d,), z_dev(d))
    for d in range(1, R):
        send(mine, kr.at[d], kr_sem, (d,), row_dev(d))

    hz = Z // 2
    W = D // SUBS
    half = SUBS // 2

    def z_rows(d):
        return pl.ds(pl.multiple_of(lax.rem(t + d + Z, Z) * rz, rz), rz)

    def z_cols(q):
        return pl.ds(q * W, W)

    def z_send(w, j, q, src):
        send(src, zr.at[w, j, :, z_cols(q)], zrs_sem, (w, j, q), z_dev(1 - 2 * w))

    def z_arrived(w, j, q):
        arrived(zr.at[w, j, :, z_cols(q)], zrs_sem, (w, j, q), z_dev(1 - 2 * w))

    firsts = (range(half), range(half, SUBS))
    for i in range(half):
        for w in range(2):
            q = firsts[w][i]
            z_send(w, 0, q, grad.at[0, z_rows((1 - 2 * w) * hz), z_cols(q)])
    if hz > 1:
        for i in range(half):
            for w in range(2):
                q = firsts[1 - w][i]
                z_send(w, 1, q, grad.at[0, z_rows((1 - 2 * w) * (hz - 1)), z_cols(q)])

    for i in range(acts.shape[1] // BLOCK):
        block = acts[:, i * BLOCK:(i + 1) * BLOCK].astype(f32)
        acts_t[i] = block.T.astype(bf16)
    xr[:, K] = jnp.zeros((R, rr, BLOCK), bf16)
    for i in range(Z):
        rows = pl.ds(pl.multiple_of(i * rz, rz), rz)
        pltpu.make_async_copy(grad.at[0, rows, :], own.at[rows, :], own_sem.at[i]).wait()

    ids = lax.broadcasted_iota(i32, tab.shape, 0) * BLOCK + lax.broadcasted_iota(i32, tab.shape, 1)

    def to_smem(src, dst, i):
        copy = pltpu.make_async_copy(src, dst, loc_sem.at[i])
        copy.start()
        copy.wait()

    def marks_first():
        kz[0] = mine[...]
        kr[0] = mine[...]
        for d in range(1, Z):
            arrived(kz.at[d], kz_sem, (d,), z_dev(-d))
        for d in range(1, R):
            arrived(kr.at[d], kr_sem, (d,), row_dev(-d))
        to_smem(kz, kz_s, 0)
        to_smem(kr, kr_s, 1)

        def mark(k, m):
            for d in range(R):
                m = jnp.where(ids == kr_s[d, 0, k], 1, m)
            return m

        marks[y] = lax.fori_loop(0, K, mark, jnp.zeros(tab.shape, i32))

    hy = Y // 2

    def marks_step(j):
        if j > 0:
            for w in range(2):
                if w == 0 or j < hy:
                    place = lax.rem(y - (1 - 2 * w) * j + Y, Y)
                    arrived(marks.at[place], mk_sem, (w, j - 1), y_dev(1 - 2 * w))
        for w in range(2):
            if j < hy and (w == 0 or j < hy - 1):
                place = lax.rem(y - (1 - 2 * w) * j + Y, Y)
                send(marks.at[place], marks.at[place], mk_sem, (w, j), y_dev(1 - 2 * w))

    def places():
        m = marks[0]
        for i in range(1, Y):
            m = jnp.maximum(m, marks[i])
        lane = lax.broadcasted_iota(i32, tab.shape, 1)
        sub = lax.broadcasted_iota(i32, tab.shape, 0)
        run = m
        step = 1
        while step < BLOCK:
            run = run + jnp.where(lane >= step, pltpu.roll(run, step, 1), 0)
            step *= 2
        total = jnp.broadcast_to(run[:, BLOCK - 1:BLOCK], tab.shape)
        above = total
        step = 1
        while step < tab.shape[0]:
            above = above + jnp.where(sub >= step, pltpu.roll(above, step, 0), 0)
            step *= 2
        count = run + above - total - m
        tab[...] = count
        to_smem(tab, c_s, 2)

        def region(o, carry):
            base, before = carry
            first = starts[0, o]
            inside = ids >= first
            there = c_s[first >> 7, first & 127]
            return jnp.where(inside, o * POOL, base), jnp.where(inside, there, before)

        zero = jnp.zeros(tab.shape, i32)
        base, before = lax.fori_loop(0, owners, region, (zero, zero))
        tab[...] = base + count - before
        to_smem(tab, p_s, 3)

    def place_of(d, k):
        block = kr_s[d, 0, k]
        return p_s[block >> 7, block & 127]

    def sources():
        at = lax.broadcasted_iota(i32, (8, BLOCK), 0) * BLOCK + lax.broadcasted_iota(i32, (8, BLOCK), 1)
        for d in range(R):
            def fill(k, row):
                return jnp.where(at == place_of(d, k), k, row)

            srcv[d] = lax.fori_loop(0, K, fill, jnp.full((8, BLOCK), K, i32))
        to_smem(srcv, src_s, 4)

    order = (tuple(firsts[1]) + tuple(firsts[0]), tuple(firsts[0]) + tuple(firsts[1]))
    CH = min(512, W)

    def z_add(w, j, q, d):
        rows = z_rows(d)

        def add(c, _):
            at = pl.ds(pl.multiple_of(q * W + c * CH, CH), CH)
            zr[w, j, :, at] = (zr[w, j, :, at].astype(f32) + own[rows, at].astype(f32)).astype(bf16)
            return 0

        lax.fori_loop(0, W // CH, add, 0)

    marks_first()
    marks_step(0)
    for j in range(1, hz):
        for i in range(SUBS):
            for w in range(2):
                q = order[w][i]
                if j == 1 and q not in firsts[w]:
                    continue
                z_arrived(w, j - 1, q)
                z_add(w, j - 1, q, (1 - 2 * w) * (hz - j))
                z_send(w, j, q, zr.at[w, j - 1, :, z_cols(q)])
        if j <= hy:
            marks_step(j)
    for j in range(max(hz, 1), hy + 1):
        marks_step(j)
    places()
    sources()
    mine_rows = z_rows(0)
    for q in range(SUBS):
        for w in range(2):
            if hz > 1 or q in firsts[w]:
                z_arrived(w, hz - 1, q)

        def total_cols(c, _):
            at = pl.ds(pl.multiple_of(q * W + c * CH, CH), CH)
            sum_ = own[mine_rows, at].astype(f32)
            for w in range(2):
                if hz > 1 or q in firsts[w]:
                    sum_ = sum_ + zr[w, hz - 1, :, at].astype(f32)
            for i in range(CH // BLOCK):
                gsum[q * (W // BLOCK) + c * (CH // BLOCK) + i] = sum_[:, i * BLOCK:(i + 1) * BLOCK].astype(bf16)
            return 0

        lax.fori_loop(0, W // CH, total_cols, 0)

    far = sorted(range(1, Z), key=lambda d: -min(d, Z - d))
    for b in range(BATCHES):
        batch = pl.ds(b * KB, KB)
        for d in far:
            def put(i, _):
                col = lax.rem(kz_s[(Z - d) % Z, 0, b * KB + i], cols)
                pack[d, b * KB + i] = gsum[col]
                return 0

            lax.fori_loop(0, KB, put, 0)
            send(pack.at[d, batch], gsel.at[t, batch], za_sem, (d, b), z_dev(d))

        def keep(i, _):
            col = lax.rem(kz_s[0, 0, b * KB + i], cols)
            gsel[t, b * KB + i] = gsum[col]
            return 0

        lax.fori_loop(0, KB, keep, 0)

    for b in range(BATCHES):
        batch = pl.ds(b * KB, KB)
        for d in far:
            arrived(gsel.at[lax.rem(t - d + Z, Z), batch], za_sem, (d, b), z_dev(-d))

        def tile(i, _):
            k = b * KB + i
            left = acts_t[lax.div(kr_s[0, 0, k], cols)]
            right = gsel[:, k].reshape(BLOCK, BLOCK)
            product = jnp.dot(left, right, preferred_element_type=f32).astype(bf16)
            tiles[:, k] = product.reshape(R, rr, BLOCK)
            xr[0, k] = tiles[s, k]
            return 0

        lax.fori_loop(0, KB, tile, 0)
        for d in range(1, R):
            send(tiles.at[lax.rem(s + d, R), batch], xr.at[d, batch], xa_sem, (d, b), row_dev(d))
    for b in range(BATCHES):
        for d in range(1, R):
            arrived(xr.at[d, pl.ds(b * KB, KB)], xa_sem, (d, b), row_dev(-d))

    HS = SL // 2

    def y_at(d, p):
        return lax.rem(y + d + Y, Y) * SL + p

    def slot_sum(place):
        sum_ = jnp.zeros((rr, BLOCK), f32)
        for d in range(R):
            sum_ = sum_ + xr[d, src_s[d, place >> 7, place & 127]].astype(f32)
        return sum_

    def y_send(w, j, h, src):
        send(src, yr.at[w, j, pl.ds(h * HS, HS)], yrs_sem, (w, j, h), y_dev(1 - 2 * w))

    def y_arrived(w, j, h):
        arrived(yr.at[w, j, pl.ds(h * HS, HS)], yrs_sem, (w, j, h), y_dev(1 - 2 * w))

    def y_first(w, j, h):
        def one(p, _):
            ys[w, j, p] = slot_sum(y_at((1 - 2 * w) * (hy - j), h * HS + p)).astype(bf16)
            return 0

        lax.fori_loop(0, HS, one, 0)
        y_send(w, j, h, ys.at[w, j])

    for w in range(2):
        y_first(w, 0, w)
    if hy > 1:
        for w in range(2):
            y_first(w, 1, 1 - w)
    for j in range(1, hy):
        for i in range(2):
            for w in range(2):
                h = (1 - w, w)[i]
                if j == 1 and h != w:
                    continue
                y_arrived(w, j - 1, h)

                def one(p, _):
                    slot = h * HS + p
                    there = slot_sum(y_at((1 - 2 * w) * (hy - j), slot))
                    yr[w, j - 1, slot] = (yr[w, j - 1, slot].astype(f32) + there).astype(bf16)
                    return 0

                lax.fori_loop(0, HS, one, 0)
                y_send(w, j, h, yr.at[w, j - 1, pl.ds(h * HS, HS)])
    def own_sum(p, _):
        tot[p] = slot_sum(y_at(0, p))
        return 0

    lax.fori_loop(0, SL, own_sum, 0)
    for h in range(2):
        for w in range(2):
            if hy > 1 or h == w:
                y_arrived(w, hy - 1, h)
    sub8 = lax.broadcasted_iota(i32, (8, BLOCK), 0)
    energy = jnp.zeros((8, BLOCK), f32)
    for h in range(2):
        def squares(g, energy):
            here = jnp.zeros((rr, BLOCK), f32)
            for i in range(POOL):
                p = g * POOL + i
                value = tot[p]
                for w in range(2):
                    if hy > 1 or h == w:
                        value = value + yr[w, hy - 1, p].astype(f32)
                tot[p] = value
                here = here + value * value
            line = jnp.sum(here, axis=0, keepdims=True)
            return jnp.where(sub8 == g, line, energy)

        energy = lax.fori_loop(h * (R // 2), (h + 1) * (R // 2), squares, energy)
    eb[0] = energy
    for d in range(1, R):
        send(eb.at[0], eb.at[d], e_sem, (d,), row_dev(d))
    count = jnp.zeros((8, BLOCK), i32)
    for g in range(R):
        o = y * R + g
        first = starts[0, o]
        after = starts[0, jnp.minimum(o + 1, owners - 1)]
        after = jnp.where(o + 1 < owners, after, NB)
        n = c_s[after >> 7, after & 127] - c_s[first >> 7, first & 127]
        count = jnp.where(sub8 == g, n, count)
    for d in range(1, R):
        arrived(eb.at[d], e_sem, (d,), row_dev(-d))
        energy = energy + eb[d]
    count = jnp.maximum(count, 1).astype(f32)
    mean_sq = jnp.sum(energy, axis=1, keepdims=True) / (count * (BLOCK * BLOCK))
    fac[...] = lax.rsqrt(mean_sq + epsilon)

    def scale(p, _):
        full[y * SL + p] = (tot[p] * fac[pl.ds(p >> 2, 1), :]).astype(bf16)
        return 0

    def ag_part(w, j, h):
        return full.at[pl.ds(y_at(-(1 - 2 * w) * j, h * HS), HS)]

    def ag_send(w, j, h):
        send(ag_part(w, j, h), ag_part(w, j, h), yag_sem, (w, j, h), y_dev(1 - 2 * w))

    for h in range(2):
        lax.fori_loop(h * HS, (h + 1) * HS, scale, 0)
        for w in range(2):
            if hy > 1 or h == w:
                ag_send(w, 0, h)
    for j in range(1, hy + 1):
        for h in range(2):
            for w in range(2):
                if j == hy and h != w:
                    continue
                arrived(ag_part(w, j, h), yag_sem, (w, j - 1, h), y_dev(1 - 2 * w))
                if j < hy - 1 or (j == hy - 1 and h == w):
                    ag_send(w, j, h)

    slice_ = pl.ds(pl.multiple_of(s * rr, rr), rr)
    near = sorted(range(1, R), key=lambda d: -min(d, R - d))
    for b in range(BATCHES):
        batch = pl.ds(b * KB, KB)
        for d in near:
            def put(i, _):
                k = b * KB + i
                opack[d, k] = full[place_of((R - d) % R, k)]
                return 0

            lax.fori_loop(0, KB, put, 0)
            send(opack.at[d, batch], out.at[batch, slice_, :], ret_sem, (d, b), row_dev(d))

    def keep_own(k, _):
        out[k, slice_, :] = full[place_of(0, k)]
        return 0

    lax.fori_loop(0, K, keep_own, 0)
    for b in range(BATCHES):
        for d in near:
            rows = pl.ds(pl.multiple_of(lax.rem(s - d + R, R) * rr, rr), rr)
            arrived(out.at[pl.ds(b * KB, KB), rows, :], ret_sem, (d, b), row_dev(-d))
    for copy in pending:
        copy.wait_send()


def shards(R, Z, grad_terms, acts, kept, starts):
    Y = lax.axis_size("dp") // R
    tokens, D = grad_terms.shape[1:]
    K = kept.shape[2]
    NB = (acts.shape[1] // BLOCK) * (D // BLOCK)
    rz, rr = BLOCK // Z, BLOCK // R
    SL = POOL * R
    hz, hy = Z // 2, Y // 2
    tab = (-(-(NB // BLOCK + 1) // 8) * 8, BLOCK)
    vmem, smem, dma = pltpu.VMEM, pltpu.SMEM, pltpu.SemaphoreType.DMA
    in_vmem = pl.BlockSpec(memory_space=pltpu.VMEM)
    result = pl.pallas_call(
        functools.partial(body, Y, R, Z, NB),
        out_shape=jax.ShapeDtypeStruct((K, BLOCK, BLOCK), bf16),
        in_specs=[
            pl.BlockSpec(memory_space=pl.ANY),
            in_vmem,
            in_vmem,
            pl.BlockSpec(memory_space=pltpu.SMEM),
        ],
        out_specs=in_vmem,
        scratch_shapes=[
            vmem((tokens, D), bf16),
            vmem((2, hz, rz, D), bf16),
            vmem((D // BLOCK, rz, BLOCK), bf16),
            vmem((Z, K, rz, BLOCK), bf16),
            vmem((Z, K, rz, BLOCK), bf16),
            vmem((acts.shape[1] // BLOCK, BLOCK, BLOCK), bf16),
            vmem((R, K, rr, BLOCK), bf16),
            vmem((R, K + 1, rr, BLOCK), bf16),
            vmem((2, 2, SL // 2, rr, BLOCK), bf16),
            vmem((2, hy, SL, rr, BLOCK), bf16),
            vmem((SL, rr, BLOCK), f32),
            vmem((R, 8, BLOCK), f32),
            vmem((8, BLOCK), f32),
            vmem((Y * SL, rr, BLOCK), bf16),
            vmem((R, K, rr, BLOCK), bf16),
            vmem((8, BLOCK), i32),
            vmem((Z, 8, BLOCK), i32),
            vmem((R, 8, BLOCK), i32),
            vmem((Y,) + tab, i32),
            vmem(tab, i32),
            vmem((R, 8, BLOCK), i32),
            smem((Z, 8, BLOCK), i32),
            smem((R, 8, BLOCK), i32),
            smem(tab, i32),
            smem(tab, i32),
            smem((R, 8, BLOCK), i32),
            dma((Z,)),
            dma((2, Z)),
            dma((2, R)),
            dma((2, 2, hy)),
            dma((5,)),
            dma((2, 2, hz, SUBS)),
            dma((2, Z, BATCHES)),
            dma((2, R, BATCHES)),
            dma((2, 2, hy, 2)),
            dma((2, R)),
            dma((2, 2, hy, 2)),
            dma((2, R, BATCHES)),
        ],
        compiler_params=pltpu.CompilerParams(
            collective_id=0, has_side_effects=True, vmem_limit_bytes=40 * 1024 * 1024
        ),
    )(grad_terms, acts, kept[0], starts)
    return result[None, None]


def solution(mesh, row=ROW):
    placed = (
        P("tensor", "dp", None),
        P("dp", "tensor"),
        P("dp", "tensor", None),
        P("tensor", None),
    )
    return jax.shard_map(
        functools.partial(shards, row, mesh.shape["tensor"]),
        mesh=mesh,
        in_specs=placed,
        out_specs=P("dp", "tensor", None, None, None),
        check_vma=False,
    )
```

```python
import functools

import jax
import jax.numpy as jnp
from jax import lax
from jax.experimental import pallas as pl
from jax.experimental.pallas import tpu as pltpu
from jax.sharding import PartitionSpec as P

BLOCK = 128
POOL = 4
ROW = 8
SUBS = 4
PARTS = 4
UNROLL = 8

epsilon = 1e-06
MESH = pl.DeviceIdType.MESH
f32, bf16, i32 = jnp.float32, jnp.bfloat16, jnp.int32


def body(
    Y, R, Z, NB,
    grad, acts_in, kept_in, starts_in, out,
    acts, kept, kept_s, starts, own, zr, gsum, pack, gsel, acts_t, perm, tiles, fwd, mid, xs, sel, tot,
    esq, eb, ey, fac, facs, full, back, opack, land, mine, kz, mr, my, pr, py, tab, square,
    kz_s, c_s, p_s, fac_s,
    in_sem, own_sem, kz_sem, mr_sem, my_sem, pr_sem, py_sem, loc_sem, zrs_sem, za_sem, xa_sem, ya_sem,
    er_sem, ey_sem, yag_sem, ret_sem,
):
    dp, t = lax.axis_index("dp"), lax.axis_index("tensor")
    y, s = dp // R, lax.rem(dp, R)
    K = out.shape[0]
    D = own.shape[1]
    rz, J = BLOCK // Z, BLOCK // (Y * R)
    cols = D // BLOCK
    KB = Y
    batches = K // KB
    H = KB * J
    RJ = R * J
    owners = Y * R
    SR = POOL * owners * J
    pending = []

    def z_dev(d):
        return (dp, lax.rem(t + d + Z, Z))

    def row_dev(d):
        return (y * R + lax.rem(s + d + R, R), t)

    def y_dev(d):
        return (lax.rem(y + d + Y, Y) * R + s, t)

    def send(src, dst, sems, index, device):
        copy = pltpu.make_async_remote_copy(
            src_ref=src, dst_ref=dst,
            send_sem=sems.at[(0,) + index], recv_sem=sems.at[(1,) + index],
            device_id=device, device_id_type=MESH,
        )
        copy.start()
        pending.append(copy)

    def arrived(dst, sems, index, device):
        pltpu.make_async_remote_copy(
            src_ref=dst, dst_ref=dst,
            send_sem=sems.at[(0,) + index], recv_sem=sems.at[(1,) + index],
            device_id=device, device_id_type=MESH,
        ).wait_recv()

    def loop(n, step):
        def one(i, _):
            step(i)
            return 0

        lax.fori_loop(0, n, one, 0, unroll=min(UNROLL, n))

    barrier = pltpu.get_barrier_semaphore()
    partners = [z_dev(d) for d in range(1, Z)] + [row_dev(d) for d in range(1, R)]
    partners += [y_dev(d) for d in range(1, Y)]
    for device in partners:
        pl.semaphore_signal(barrier, inc=1, device_id=device, device_id_type=MESH)
    inputs = [
        pltpu.make_async_copy(src, dst, in_sem.at[i])
        for i, (src, dst) in enumerate(((kept_in.at[0], kept), (kept_in.at[0], kept_s), (starts_in, starts), (acts_in, acts)))
    ]
    for copy in inputs:
        copy.start()
    for i in range(Z):
        rows = pl.ds(pl.multiple_of(i * rz, rz), rz)
        pltpu.make_async_copy(grad.at[0, rows, :], own.at[rows, :], own_sem.at[i]).start()
    inputs[0].wait()
    mine[...] = jnp.full(mine.shape, -1, i32)
    mine[0:1, 0:K] = kept[...]
    pl.semaphore_wait(barrier, len(partners))

    for d in range(1, Z):
        send(mine, kz.at[d], kz_sem, (d,), z_dev(d))

    hz = Z // 2
    W = D // SUBS
    half = SUBS // 2

    def z_rows(d):
        return pl.ds(pl.multiple_of(lax.rem(t + d + Z, Z) * rz, rz), rz)

    def z_cols(q):
        return pl.ds(q * W, W)

    def z_send(w, j, q, src):
        send(src, zr.at[w, j, :, z_cols(q)], zrs_sem, (w, j, q), z_dev(1 - 2 * w))

    def z_arrived(w, j, q):
        arrived(zr.at[w, j, :, z_cols(q)], zrs_sem, (w, j, q), z_dev(1 - 2 * w))

    firsts = (range(half), range(half, SUBS))
    for i in range(half):
        for w in range(2):
            q = firsts[w][i]
            z_send(w, 0, q, grad.at[0, z_rows((1 - 2 * w) * hz), z_cols(q)])
    if hz > 1:
        for i in range(half):
            for w in range(2):
                q = firsts[1 - w][i]
                z_send(w, 1, q, grad.at[0, z_rows((1 - 2 * w) * (hz - 1)), z_cols(q)])

    for copy in inputs[1:]:
        copy.wait()
    ids = lax.broadcasted_iota(i32, tab.shape, 0) * BLOCK + lax.broadcasted_iota(i32, tab.shape, 1)

    def mark(k, m):
        return jnp.where(ids == kept_s[0, k], 1, m)

    mr[0] = lax.fori_loop(0, K, mark, jnp.zeros(tab.shape, i32), unroll=min(UNROLL, K))
    for d in range(1, R):
        send(mr.at[0], mr.at[d], mr_sem, (d,), row_dev(d))
    for i in range(acts.shape[1] // BLOCK):
        block = acts[:, i * BLOCK:(i + 1) * BLOCK].astype(f32)
        acts_t[i] = block.T.astype(bf16)
    to = lax.broadcasted_iota(i32, (BLOCK, BLOCK), 0)
    frm = lax.broadcasted_iota(i32, (BLOCK, BLOCK), 1)
    for i, (outer, inner) in enumerate(((R, KB), (KB, R))):
        a, b, c = lax.div(to, inner * J), lax.rem(lax.div(to, J), inner), lax.rem(to, J)
        perm[i] = jnp.where(frm == (b * outer + a) * J + c, 1.0, 0.0).astype(bf16)
    for i in range(Z):
        rows = pl.ds(pl.multiple_of(i * rz, rz), rz)
        pltpu.make_async_copy(grad.at[0, rows, :], own.at[rows, :], own_sem.at[i]).wait()

    def to_smem(src, dst, i):
        copy = pltpu.make_async_copy(src, dst, loc_sem.at[i])
        copy.start()
        copy.wait()

    def gathered(ref, sems, dev, n):
        for d in range(1, n):
            arrived(ref.at[d], sems, (d,), dev(-d))
        m = ref[0]
        for d in range(1, n):
            m = jnp.maximum(m, ref[d])
        return m

    def marks_row():
        kz[0] = mine[...]
        for d in range(1, Z):
            arrived(kz.at[d], kz_sem, (d,), z_dev(-d))
        to_smem(kz, kz_s, 0)
        my[0] = gathered(mr, mr_sem, row_dev, R)
        for d in range(1, Y):
            send(my.at[0], my.at[d], my_sem, (d,), y_dev(d))

    def places():
        m = gathered(my, my_sem, y_dev, Y)
        lane = lax.broadcasted_iota(i32, tab.shape, 1)
        sub = lax.broadcasted_iota(i32, tab.shape, 0)
        run = m
        step = 1
        while step < BLOCK:
            run = run + jnp.where(lane >= step, pltpu.roll(run, step, 1), 0)
            step *= 2
        total = jnp.broadcast_to(run[:, BLOCK - 1:BLOCK], tab.shape)
        above = total
        step = 1
        while step < tab.shape[0]:
            above = above + jnp.where(sub >= step, pltpu.roll(above, step, 0), 0)
            step *= 2
        count = run + above - total - m
        tab[...] = count
        to_smem(tab, c_s, 1)

        def region(o, carry):
            base, before = carry
            first = starts[0, o]
            inside = ids >= first
            there = c_s[first >> 7, first & 127]
            return jnp.where(inside, o * POOL, base), jnp.where(inside, there, before)

        zero = jnp.zeros(tab.shape, i32)
        base, before = lax.fori_loop(0, owners, region, (zero, zero), unroll=UNROLL)
        tab[...] = base + count - before
        to_smem(tab, p_s, 2)

        sub8 = lax.broadcasted_iota(i32, (8, BLOCK), 0)
        lane8 = lax.broadcasted_iota(i32, (8, BLOCK), 1)

        def fill(k, tile):
            here = (sub8 == lax.div(k, KB)) & (lax.div(lane8, J) == s * KB + lax.rem(k, KB))
            return jnp.where(here, place_of(k) * J + lax.rem(lane8, J), tile)

        pr[0] = lax.fori_loop(0, K, fill, jnp.full((8, BLOCK), -1, i32), unroll=min(UNROLL, K))
        for d in range(1, R):
            send(pr.at[0], pr.at[d], pr_sem, (d,), row_dev(d))

    def place_of(k):
        block = kept_s[0, k]
        return p_s[block >> 7, block & 127]

    def places_row():
        py[y] = gathered(pr, pr_sem, row_dev, R)
        for d in range(1, Y):
            send(py.at[y], py.at[y], py_sem, (d,), y_dev(d))
        square[...] = jnp.zeros(square.shape, f32)
        square[0:8, :] = py[y].astype(f32)
        turned = square[...].T
        lane = lax.broadcasted_iota(i32, (BLOCK, SR), 1).astype(f32)
        for b in range(batches):
            back[b * BLOCK:(b + 1) * BLOCK, :] = jnp.where(turned[:, b:b + 1] == lane, 1.0, 0.0).astype(bf16)

    def places_all():
        for d in range(1, Y):
            arrived(py.at[lax.rem(y - d + Y, Y)], py_sem, (d,), y_dev(-d))

    def select(b):
        row = lax.broadcasted_iota(i32, (SR, BLOCK), 0)

        def one(i, _):
            at = pl.ds(pl.multiple_of(i * BLOCK, BLOCK), BLOCK)
            sel[b, :, at] = jnp.where(py[i][b:b + 1, :] == row, 1.0, 0.0).astype(bf16)
            return 0

        lax.fori_loop(0, Y, one, 0)

    def counts():
        lane = lax.broadcasted_iota(i32, (8, BLOCK), 1)

        def one(o, n):
            first = starts[0, o]
            after = starts[0, jnp.minimum(o + 1, owners - 1)]
            after = jnp.where(o + 1 < owners, after, NB)
            there = c_s[after >> 7, after & 127] - c_s[first >> 7, first & 127]
            return jnp.where(lane == o, there, n)

        n = lax.fori_loop(0, owners, one, jnp.ones((8, BLOCK), i32), unroll=UNROLL)
        fac[...] = jnp.maximum(n, 1).astype(f32)

    order = (tuple(firsts[1]) + tuple(firsts[0]), tuple(firsts[0]) + tuple(firsts[1]))
    CH = min(512, W)

    def z_add(w, j, q, d):
        rows = z_rows(d)

        def add(c):
            at = pl.ds(pl.multiple_of(q * W + c * CH, CH), CH)
            zr[w, j, :, at] = (zr[w, j, :, at].astype(f32) + own[rows, at].astype(f32)).astype(bf16)

        loop(W // CH, add)

    chores = [marks_row, places, places_row, places_all] + [functools.partial(select, b) for b in range(batches)] + [counts]
    for j in range(1, hz):
        for i in range(SUBS):
            for w in range(2):
                q = order[w][i]
                if j == 1 and q not in firsts[w]:
                    continue
                z_arrived(w, j - 1, q)
                z_add(w, j - 1, q, (1 - 2 * w) * (hz - j))
                z_send(w, j, q, zr.at[w, j - 1, :, z_cols(q)])
            if chores and (i % 2 or j == hz - 1) and (j > 1 or i == SUBS - 1):
                chores.pop(0)()
    for chore in chores:
        chore()
    mine_rows = z_rows(0)
    for q in range(SUBS):
        for w in range(2):
            if hz > 1 or q in firsts[w]:
                z_arrived(w, hz - 1, q)

        def total_cols(c):
            at = pl.ds(pl.multiple_of(q * W + c * CH, CH), CH)
            sum_ = own[mine_rows, at].astype(f32)
            for w in range(2):
                if hz > 1 or q in firsts[w]:
                    sum_ = sum_ + zr[w, hz - 1, :, at].astype(f32)
            for i in range(CH // BLOCK):
                gsum[q * (W // BLOCK) + c * (CH // BLOCK) + i] = sum_[:, i * BLOCK:(i + 1) * BLOCK].astype(bf16)

        loop(W // CH, total_cols)

    far = sorted(range(1, Z), key=lambda d: -min(d, Z - d))
    for b in range(batches):
        batch = pl.ds(b * KB, KB)
        for d in far:
            def put(i):
                col = lax.rem(kz_s[(Z - d) % Z, 0, b * KB + i], cols)
                pack[d, b * KB + i] = gsum[col]

            loop(KB, put)
            send(pack.at[d, batch], gsel.at[t, batch], za_sem, (d, b), z_dev(d))

        def keep(i):
            col = lax.rem(kz_s[0, 0, b * KB + i], cols)
            gsel[t, b * KB + i] = gsum[col]

        loop(KB, keep)

    for b in range(batches):
        batch = pl.ds(b * KB, KB)
        for d in far:
            arrived(gsel.at[lax.rem(t - d + Z, Z), batch], za_sem, (d, b), z_dev(-d))
        for i in range(KB):
            k = b * KB + i
            left = acts_t[lax.div(kept_s[0, k], cols)]
            right = gsel[:, k].reshape(BLOCK, BLOCK)
            product = jnp.dot(left, right, preferred_element_type=f32).astype(bf16)
            tiles[:, i] = product.reshape(Y, RJ, BLOCK)
        for i in range(Y):
            turned = jnp.dot(perm[0], tiles[i].reshape(BLOCK, BLOCK), preferred_element_type=f32)
            fwd[b, :, i] = turned.astype(bf16).reshape(R, H, BLOCK)
        for d in range(1, R):
            send(fwd.at[b, lax.rem(s + d, R)], mid.at[b, :, s], xa_sem, (d, b), row_dev(d))
        mid[b, :, s] = fwd[b, s]
        for d in range(1, R):
            arrived(mid.at[b, :, lax.rem(s - d + R, R)], xa_sem, (d, b), row_dev(-d))
        for d in sorted(range(1, Y), key=lambda d: -min(d, Y - d)):
            send(mid.at[b, lax.rem(y + d, Y)], xs.at[b, y], ya_sem, (d, b), y_dev(d))
        xs[b, y] = mid[b, y]

    for b in range(batches):
        for d in range(1, Y):
            arrived(xs.at[b, lax.rem(y - d + Y, Y)], ya_sem, (d, b), y_dev(-d))
        here = jnp.dot(sel[b], xs[b].reshape(Y * BLOCK, BLOCK), preferred_element_type=f32)
        tot[...] = here if b == 0 else tot[...] + here

    hy = Y // 2
    HS = SR // PARTS
    firsts = (range(PARTS // 2), range(PARTS // 2, PARTS))

    def y_of(d):
        return lax.rem(y + d + Y, Y)

    def ag_part(d, h):
        return full.at[y_of(d), pl.ds(h * HS, HS)]

    def ag_send(w, j, h):
        away = 1 - 2 * w
        if j < hy - 1:
            send(ag_part(-away * j, h), ag_part(-away * j, h), yag_sem, (w, j, h), y_dev(away))
        if j == hy - 2 and h in firsts[w]:
            send(ag_part(-away * j, h), ag_part(-away * j, h), yag_sem, (w, hy - 1, h), y_dev(2 * away))

    full[y] = tot[...].astype(bf16)
    for i in range(PARTS):
        for w in range(2):
            ag_send(w, 0, (i if w == 0 else PARTS - 1 - i))
    squares = jnp.sum((tot[...] * tot[...]).reshape(owners, POOL * J, BLOCK), axis=1)
    esq[...] = jnp.zeros(esq.shape, f32)
    esq[0:owners, :] = squares
    eb[0] = lax.dot_general(
        jnp.ones((8, BLOCK), f32), esq[...], (((1,), (1,)), ((), ())),
        precision=lax.Precision.HIGHEST, preferred_element_type=f32,
    )
    for d in range(1, R):
        send(eb.at[0], eb.at[d], er_sem, (d,), row_dev(d))

    near = sorted(range(1, R), key=lambda d: -min(d, R - d))

    def give(d):
        at = y_of(d)
        rows = jnp.dot(back[...], full[at], preferred_element_type=f32).astype(bf16)
        opack[at] = rows.reshape(batches, R, H, BLOCK)
        for e in near:
            send(opack.at[at, :, lax.rem(s + e, R)], land.at[at, :, s], ret_sem, (e, d % Y), row_dev(e))
        land[at, :, s] = opack[at, :, s]

    def finish(d):
        at = y_of(d)
        for e in near:
            arrived(land.at[at, :, lax.rem(s - e + R, R)], ret_sem, (e, d % Y), row_dev(-e))
        rows = pl.ds(pl.multiple_of(at * RJ, RJ), RJ)
        for b in range(batches):
            turned = jnp.dot(perm[1], land[at, b].reshape(BLOCK, BLOCK), preferred_element_type=f32)
            turned = turned.reshape(KB, RJ, BLOCK)
            for i in range(KB):
                k = b * KB + i
                out[k, rows, :] = (turned[i] * facs[k:k + 1, :]).astype(bf16)

    def energies(ref, sems, dev, n):
        sum_ = ref[0]
        for d in range(1, n):
            arrived(ref.at[d], sems, (d,), dev(-d))
            sum_ = sum_ + ref[d]
        return sum_

    def energy_row():
        ey[0] = energies(eb, er_sem, row_dev, R)
        for d in range(1, Y):
            send(ey.at[0], ey.at[d], ey_sem, (d,), y_dev(d))

    def factors():
        mean_sq = energies(ey, ey_sem, y_dev, Y) / (fac[...] * (BLOCK * BLOCK))
        fac[...] = lax.rsqrt(mean_sq + epsilon)
        to_smem(fac, fac_s, 3)

        def one(k):
            facs[pl.ds(k, 1), :] = jnp.full((1, BLOCK), fac_s[0, place_of(k) >> 2], f32)

        loop(K, one)

    give(0)
    energy_row()
    waiting = [0]
    for j in range(1, hy + 1):
        for i in range(PARTS):
            for w in range(2):
                h = i if w == 0 else PARTS - 1 - i
                if j == hy and h not in firsts[w]:
                    continue
                hop = 2 if j == hy else 1
                arrived(ag_part(-(1 - 2 * w) * j, h), yag_sem, (w, j - 1, h), y_dev(-(1 - 2 * w) * hop))
                if j < hy:
                    ag_send(w, j, h)
        come = (-j, j) if j < hy else (j,)
        for d in come:
            give(d)
        if j == 2:
            factors()
        if j > 2:
            for d in waiting[:2]:
                finish(d)
            waiting = waiting[2:]
        waiting += come
    for d in waiting:
        finish(d)
    for copy in pending:
        copy.wait_send()


def shards(R, Z, grad_terms, acts, kept, starts):
    Y = lax.axis_size("dp") // R
    tokens, D = grad_terms.shape[1:]
    K = kept.shape[2]
    NB = (acts.shape[1] // BLOCK) * (D // BLOCK)
    rz = BLOCK // Z
    hz, hy = Z // 2, Y // 2
    J = BLOCK // (Y * R)
    H = Y * J
    batches = K // Y
    SR = POOL * Y * R * J
    tab = (-(-(NB // BLOCK + 1) // 8) * 8, BLOCK)
    vmem, smem, dma = pltpu.VMEM, pltpu.SMEM, pltpu.SemaphoreType.DMA
    in_vmem = pl.BlockSpec(memory_space=pltpu.VMEM)
    result = pl.pallas_call(
        functools.partial(body, Y, R, Z, NB),
        out_shape=jax.ShapeDtypeStruct((K, BLOCK, BLOCK), bf16),
        in_specs=[pl.BlockSpec(memory_space=pltpu.HBM)] * 4,
        out_specs=in_vmem,
        scratch_shapes=[
            vmem(acts.shape, bf16),
            vmem(kept.shape[1:], i32),
            smem(kept.shape[1:], i32),
            smem(starts.shape, i32),
            vmem((tokens, D), bf16),
            vmem((2, hz, rz, D), bf16),
            vmem((D // BLOCK, rz, BLOCK), bf16),
            vmem((Z, K, rz, BLOCK), bf16),
            vmem((Z, K, rz, BLOCK), bf16),
            vmem((acts.shape[1] // BLOCK, BLOCK, BLOCK), bf16),
            vmem((2, BLOCK, BLOCK), bf16),
            vmem((Y, Y, R * J, BLOCK), bf16),
            vmem((batches, R, Y, H, BLOCK), bf16),
            vmem((batches, Y, R, H, BLOCK), bf16),
            vmem((batches, Y, R, H, BLOCK), bf16),
            vmem((batches, SR, Y * BLOCK), bf16),
            vmem((SR, BLOCK), f32),
            vmem((BLOCK, BLOCK), f32),
            vmem((R, 8, BLOCK), f32),
            vmem((Y, 8, BLOCK), f32),
            vmem((8, BLOCK), f32),
            vmem((K, BLOCK), f32),
            vmem((Y, SR, BLOCK), bf16),
            vmem((batches * BLOCK, SR), bf16),
            vmem((Y, batches, R, H, BLOCK), bf16),
            vmem((Y, batches, R, H, BLOCK), bf16),
            vmem((8, BLOCK), i32),
            vmem((Z, 8, BLOCK), i32),
            vmem((R,) + tab, i32),
            vmem((Y,) + tab, i32),
            vmem((R, 8, BLOCK), i32),
            vmem((Y, 8, BLOCK), i32),
            vmem(tab, i32),
            vmem((BLOCK, BLOCK), f32),
            smem((Z, 8, BLOCK), i32),
            smem(tab, i32),
            smem(tab, i32),
            smem((8, BLOCK), f32),
            dma((4,)),
            dma((Z,)),
            dma((2, Z)),
            dma((2, R)),
            dma((2, Y)),
            dma((2, R)),
            dma((2, Y)),
            dma((4,)),
            dma((2, 2, hz, SUBS)),
            dma((2, Z, batches)),
            dma((2, R, batches)),
            dma((2, Y, batches)),
            dma((2, R)),
            dma((2, Y)),
            dma((2, 2, hy, PARTS)),
            dma((2, R, Y)),
        ],
        compiler_params=pltpu.CompilerParams(
            collective_id=0, has_side_effects=True, vmem_limit_bytes=40 * 1024 * 1024
        ),
    )(grad_terms, acts, kept, starts)
    return result[None, None]


def solution(mesh, row=ROW):
    placed = (
        P("tensor", "dp", None),
        P("dp", "tensor"),
        P("dp", "tensor", None),
        P("tensor", None),
    )
    return jax.shard_map(
        functools.partial(shards, row, mesh.shape["tensor"]),
        mesh=mesh,
        in_specs=placed,
        out_specs=P("dp", "tensor", None, None, None),
        check_vma=False,
    )
```

```python
import functools

import jax
import jax.numpy as jnp
from jax import lax
from jax.experimental import pallas as pl
from jax.experimental.pallas import tpu as pltpu
from jax.sharding import PartitionSpec as P

BLOCK = 128
POOL = 4
ROW = 8
SUBS = 4
PARTS = 2
UNROLL = 8

epsilon = 1e-06
MESH = pl.DeviceIdType.MESH
f32, bf16, i32 = jnp.float32, jnp.bfloat16, jnp.int32


def body(
    Y, R, Z, NB,
    grad, acts_in, kept_in, starts_in, out,
    acts, kept, kept_s, starts, own, zr, gsum, pack, gsel, acts_t, perm, tiles, fwd, mid, xs, sel, tot,
    esq, eb, ey, fac, facs, full, back, opack, land, mine, kz, mr, my, pr, py, tab, square,
    kz_s, c_s, p_s, fac_s,
    in_sem, own_sem, kz_sem, mr_sem, my_sem, pr_sem, py_sem, loc_sem, zrs_sem, za_sem, xa_sem, ya_sem,
    er_sem, ey_sem, yag_sem, ret_sem,
):
    dp, t = lax.axis_index("dp"), lax.axis_index("tensor")
    y, s = dp // R, lax.rem(dp, R)
    K = out.shape[0]
    D = own.shape[1]
    rz, J = BLOCK // Z, BLOCK // (Y * R)
    cols = D // BLOCK
    KB = Y
    batches = K // KB
    H = KB * J
    RJ = R * J
    owners = Y * R
    SR = POOL * owners * J
    pending = []

    def z_dev(d):
        return (dp, lax.rem(t + d + Z, Z))

    def row_dev(d):
        return (y * R + lax.rem(s + d + R, R), t)

    def y_dev(d):
        return (lax.rem(y + d + Y, Y) * R + s, t)

    chips = Y * R // 2
    chip, core = dp // 2, lax.rem(dp, 2)
    twin = (2 * chip + 1 - core, t)

    def chip_of(i):
        return lax.rem(chip + i, chips)

    def chip_dev(i):
        return (2 * chip_of(i) + core, t)

    def send(src, dst, sems, index, device):
        copy = pltpu.make_async_remote_copy(
            src_ref=src, dst_ref=dst,
            send_sem=sems.at[(0,) + index], recv_sem=sems.at[(1,) + index],
            device_id=device, device_id_type=MESH,
        )
        copy.start()
        pending.append(copy)

    def sent(copies):
        for copy in copies:
            copy.wait_send()

    def arrived(dst, sems, index, device):
        pltpu.make_async_remote_copy(
            src_ref=dst, dst_ref=dst,
            send_sem=sems.at[(0,) + index], recv_sem=sems.at[(1,) + index],
            device_id=device, device_id_type=MESH,
        ).wait_recv()

    def loop(n, step):
        def one(i, _):
            step(i)
            return 0

        lax.fori_loop(0, n, one, 0, unroll=min(UNROLL, n))

    barrier = pltpu.get_barrier_semaphore()
    partners = [z_dev(d) for d in range(1, Z)] + [twin] + [row_dev(2 * d + 1 - 2 * core) for d in range(1, R // 2)]
    for device in partners:
        pl.semaphore_signal(barrier, inc=1, device_id=device, device_id_type=MESH)

    def greet(i, _):
        pl.semaphore_signal(barrier, inc=1, device_id=chip_dev(i), device_id_type=MESH)
        return 0

    lax.fori_loop(1, chips, greet, 0)
    inputs = [
        pltpu.make_async_copy(src, dst, in_sem.at[i])
        for i, (src, dst) in enumerate(((kept_in.at[0], kept), (kept_in.at[0], kept_s), (starts_in, starts), (acts_in, acts)))
    ]
    for copy in inputs:
        copy.start()
    for i in range(Z):
        rows = pl.ds(pl.multiple_of(i * rz, rz), rz)
        pltpu.make_async_copy(grad.at[0, rows, :], own.at[rows, :], own_sem.at[i]).start()
    pl.semaphore_wait(barrier, len(partners) + chips - 1)

    hz = Z // 2
    W = D // SUBS
    half = SUBS // 2

    def z_rows(d):
        return pl.ds(pl.multiple_of(lax.rem(t + d + Z, Z) * rz, rz), rz)

    def z_cols(q):
        return pl.ds(q * W, W)

    def z_send(w, j, q, src):
        send(src, zr.at[w, j, :, z_cols(q)], zrs_sem, (w, j, q), z_dev(1 - 2 * w))

    def z_arrived(w, j, q):
        arrived(zr.at[w, j, :, z_cols(q)], zrs_sem, (w, j, q), z_dev(1 - 2 * w))

    firsts = (range(half), range(half, SUBS))
    for i in range(half):
        for w in range(2):
            q = firsts[w][i]
            z_send(w, 0, q, grad.at[0, z_rows((1 - 2 * w) * hz), z_cols(q)])
    if hz > 1:
        for i in range(half):
            for w in range(2):
                q = firsts[1 - w][i]
                z_send(w, 1, q, grad.at[0, z_rows((1 - 2 * w) * (hz - 1)), z_cols(q)])

    for copy in inputs[1:3]:
        copy.wait()
    ids = lax.broadcasted_iota(i32, tab.shape, 0) * BLOCK + lax.broadcasted_iota(i32, tab.shape, 1)

    def mark(k, m):
        return jnp.where(ids == kept_s[0, k], 1, m)

    mr[0] = lax.fori_loop(0, K, mark, jnp.zeros(tab.shape, i32), unroll=min(UNROLL, K))
    for d in range(1, R):
        send(mr.at[0], mr.at[d], mr_sem, (d,), row_dev(d))
    inputs[0].wait()
    mine[...] = jnp.full(mine.shape, -1, i32)
    mine[0:1, 0:K] = kept[...]
    for d in range(1, Z):
        send(mine, kz.at[d], kz_sem, (d,), z_dev(d))
    for i in range(Z):
        rows = pl.ds(pl.multiple_of(i * rz, rz), rz)
        pltpu.make_async_copy(grad.at[0, rows, :], own.at[rows, :], own_sem.at[i]).wait()

    def to_smem(src, dst, i):
        copy = pltpu.make_async_copy(src, dst, loc_sem.at[i])
        copy.start()
        copy.wait()

    def gathered(ref, sems, dev, n):
        for d in range(1, n):
            arrived(ref.at[d], sems, (d,), dev(-d))
        m = ref[0]
        for d in range(1, n):
            m = jnp.maximum(m, ref[d])
        return m

    def marks_row():
        my[0] = gathered(mr, mr_sem, row_dev, R)
        for d in range(1, Y):
            send(my.at[0], my.at[d], my_sem, (d,), y_dev(d))

    def ranks():
        kz[0] = mine[...]
        for d in range(1, Z):
            arrived(kz.at[d], kz_sem, (d,), z_dev(-d))
        to_smem(kz, kz_s, 0)

    def places():
        m = gathered(my, my_sem, y_dev, Y)
        lane = lax.broadcasted_iota(i32, tab.shape, 1)
        sub = lax.broadcasted_iota(i32, tab.shape, 0)
        run = m
        step = 1
        while step < BLOCK:
            run = run + jnp.where(lane >= step, pltpu.roll(run, step, 1), 0)
            step *= 2
        total = jnp.broadcast_to(run[:, BLOCK - 1:BLOCK], tab.shape)
        above = total
        step = 1
        while step < tab.shape[0]:
            above = above + jnp.where(sub >= step, pltpu.roll(above, step, 0), 0)
            step *= 2
        count = run + above - total - m
        tab[...] = count
        to_smem(tab, c_s, 1)

        def region(o, carry):
            base, before = carry
            first = starts[0, o]
            inside = ids >= first
            there = c_s[first >> 7, first & 127]
            return jnp.where(inside, o * POOL, base), jnp.where(inside, there, before)

        zero = jnp.zeros(tab.shape, i32)
        base, before = lax.fori_loop(0, owners, region, (zero, zero), unroll=UNROLL)
        tab[...] = base + count - before
        to_smem(tab, p_s, 2)

        sub8 = lax.broadcasted_iota(i32, (8, BLOCK), 0)
        lane8 = lax.broadcasted_iota(i32, (8, BLOCK), 1)

        def fill(k, tile):
            here = (sub8 == lax.div(k, KB)) & (lax.div(lane8, J) == s * KB + lax.rem(k, KB))
            return jnp.where(here, place_of(k) * J + lax.rem(lane8, J), tile)

        pr[0] = lax.fori_loop(0, K, fill, jnp.full((8, BLOCK), -1, i32), unroll=min(UNROLL, K))
        for d in range(1, R):
            send(pr.at[0], pr.at[d], pr_sem, (d,), row_dev(d))

    def place_of(k):
        block = kept_s[0, k]
        return p_s[block >> 7, block & 127]

    def places_row():
        py[y] = gathered(pr, pr_sem, row_dev, R)
        for d in range(1, Y):
            send(py.at[y], py.at[y], py_sem, (d,), y_dev(d))

    def going_back():
        square[...] = jnp.zeros(square.shape, f32)
        square[0:8, :] = py[y].astype(f32)
        turned = square[...].T
        lane = lax.broadcasted_iota(i32, (BLOCK, SR), 1).astype(f32)
        for b in range(batches):
            back[b * BLOCK:(b + 1) * BLOCK, :] = jnp.where(turned[:, b:b + 1] == lane, 1.0, 0.0).astype(bf16)

    def places_all():
        for d in range(1, Y):
            arrived(py.at[lax.rem(y - d + Y, Y)], py_sem, (d,), y_dev(-d))

    def select(b):
        row = lax.broadcasted_iota(i32, (SR, BLOCK), 0)

        def one(i, _):
            at = pl.ds(pl.multiple_of(i * BLOCK, BLOCK), BLOCK)
            sel[b, :, at] = jnp.where(py[i][b:b + 1, :] == row, 1.0, 0.0).astype(bf16)
            return 0

        lax.fori_loop(0, Y, one, 0)

    def counts():
        lane = lax.broadcasted_iota(i32, (8, BLOCK), 1)

        def one(o, n):
            first = starts[0, o]
            after = starts[0, jnp.minimum(o + 1, owners - 1)]
            after = jnp.where(o + 1 < owners, after, NB)
            there = c_s[after >> 7, after & 127] - c_s[first >> 7, first & 127]
            return jnp.where(lane == o, there, n)

        n = lax.fori_loop(0, owners, one, jnp.ones((8, BLOCK), i32), unroll=UNROLL)
        fac[...] = jnp.maximum(n, 1).astype(f32)

    order = (tuple(firsts[1]) + tuple(firsts[0]), tuple(firsts[0]) + tuple(firsts[1]))
    CH = min(512, W)

    def z_add(w, j, q, d):
        rows = z_rows(d)

        def add(c):
            at = pl.ds(pl.multiple_of(q * W + c * CH, CH), CH)
            zr[w, j, :, at] = (zr[w, j, :, at].astype(f32) + own[rows, at].astype(f32)).astype(bf16)

        loop(W // CH, add)

    chores = {(1, SUBS - 1): marks_row, (2, 1): ranks, (2, SUBS - 1): places, (3, SUBS - 1): places_row}
    for j in range(1, hz):
        for i in range(SUBS):
            for w in range(2):
                q = order[w][i]
                if j == 1 and q not in firsts[w]:
                    continue
                z_arrived(w, j - 1, q)
                z_add(w, j - 1, q, (1 - 2 * w) * (hz - j))
                z_send(w, j, q, zr.at[w, j - 1, :, z_cols(q)])
            if (j, i) in chores:
                chores.pop((j, i))()
    for chore in chores.values():
        chore()
    mine_rows = z_rows(0)
    for q in range(SUBS):
        for w in range(2):
            if hz > 1 or q in firsts[w]:
                z_arrived(w, hz - 1, q)

        def total_cols(c):
            at = pl.ds(pl.multiple_of(q * W + c * CH, CH), CH)
            sum_ = own[mine_rows, at].astype(f32)
            for w in range(2):
                if hz > 1 or q in firsts[w]:
                    sum_ = sum_ + zr[w, hz - 1, :, at].astype(f32)
            for i in range(CH // BLOCK):
                gsum[q * (W // BLOCK) + c * (CH // BLOCK) + i] = sum_[:, i * BLOCK:(i + 1) * BLOCK].astype(bf16)

        loop(W // CH, total_cols)

    far = sorted(range(1, Z), key=lambda d: -min(d, Z - d))

    def set_up():
        inputs[3].wait()
        for i in range(acts.shape[1] // BLOCK):
            block = acts[:, i * BLOCK:(i + 1) * BLOCK].astype(f32)
            acts_t[i] = block.T.astype(bf16)
        to = lax.broadcasted_iota(i32, (BLOCK, BLOCK), 0)
        frm = lax.broadcasted_iota(i32, (BLOCK, BLOCK), 1)
        for i, (outer, inner) in enumerate(((R, KB), (KB, R))):
            a, b, c = lax.div(to, inner * J), lax.rem(lax.div(to, J), inner), lax.rem(to, J)
            perm[i] = jnp.where(frm == (b * outer + a) * J + c, 1.0, 0.0).astype(bf16)

    def selects():
        places_all()
        for b in range(batches):
            select(b)
        counts()

    early = pending[:]
    pending.clear()
    chores = [set_up, going_back, selects, functools.partial(sent, early)]
    for b in range(batches):
        batch = pl.ds(b * KB, KB)
        for d in far:
            def put(i):
                col = lax.rem(kz_s[(Z - d) % Z, 0, b * KB + i], cols)
                pack[d, b * KB + i] = gsum[col]

            loop(KB, put)
            send(pack.at[d, batch], gsel.at[t, batch], za_sem, (d, b), z_dev(d))

        def keep(i):
            col = lax.rem(kz_s[0, 0, b * KB + i], cols)
            gsel[t, b * KB + i] = gsum[col]

        loop(KB, keep)
        if chores:
            chores.pop(0)()
    for chore in chores:
        chore()

    for b in range(batches):
        batch = pl.ds(b * KB, KB)
        for d in far:
            arrived(gsel.at[lax.rem(t - d + Z, Z), batch], za_sem, (d, b), z_dev(-d))
        for i in range(KB):
            k = b * KB + i
            left = acts_t[lax.div(kept_s[0, k], cols)]
            right = gsel[:, k].reshape(BLOCK, BLOCK)
            product = jnp.dot(left, right, preferred_element_type=f32).astype(bf16)
            tiles[:, i] = product.reshape(Y, RJ, BLOCK)
        for i in range(Y):
            turned = jnp.dot(perm[0], tiles[i].reshape(BLOCK, BLOCK), preferred_element_type=f32)
            turned = turned.astype(bf16).reshape(R // 2, 2, H, BLOCK)
            for c in range(2):
                fwd[b, c, i] = turned[:, c]
        send(fwd.at[b, 1 - core], mid.at[b, :, :, core], xa_sem, (b,), twin)
        mid[b, :, :, core] = fwd[b, core]
        arrived(mid.at[b, :, :, 1 - core], xa_sem, (b,), twin)

        def direct(i, _):
            to = chip_of(i)
            pltpu.make_async_remote_copy(
                src_ref=mid.at[b, to // (R // 2), lax.rem(to, R // 2)], dst_ref=xs.at[b, pl.ds(2 * chip, 2)],
                send_sem=ya_sem.at[0, b], recv_sem=ya_sem.at[1, b],
                device_id=chip_dev(i), device_id_type=MESH,
            ).start()
            return 0

        lax.fori_loop(1, chips, direct, 0)
        pltpu.make_async_copy(
            mid.at[b, y, s // 2], xs.at[b, pl.ds(2 * chip, 2)], ya_sem.at[1, b]
        ).start()

    for b in range(batches):
        arrived(xs.at[b], ya_sem, (b,), twin)
        here = jnp.dot(sel[b], xs[b].reshape(Y * BLOCK, BLOCK), preferred_element_type=f32)
        tot[...] = here if b == 0 else tot[...] + here

    hy = Y // 2
    HS = SR // PARTS
    firsts = (range(PARTS // 2), range(PARTS // 2, PARTS))

    def y_of(d):
        return lax.rem(y + d + Y, Y)

    def ag_part(d, h):
        return full.at[y_of(d), pl.ds(h * HS, HS)]

    def ag_send(w, j, h):
        away = 1 - 2 * w
        if j < hy - 1:
            send(ag_part(-away * j, h), ag_part(-away * j, h), yag_sem, (w, j, h), y_dev(away))
        if j == hy - 2 and h in firsts[w]:
            send(ag_part(-away * j, h), ag_part(-away * j, h), yag_sem, (w, hy - 1, h), y_dev(2 * away))

    before = len(pending)
    full[y] = tot[...].astype(bf16)
    for i in range(PARTS):
        for w in range(2):
            ag_send(w, 0, (i if w == 0 else PARTS - 1 - i))
    squares = jnp.sum((tot[...] * tot[...]).reshape(owners, POOL * J, BLOCK), axis=1)
    esq[...] = jnp.zeros(esq.shape, f32)
    esq[0:owners, :] = squares
    eb[0] = lax.dot_general(
        jnp.ones((8, BLOCK), f32), esq[...], (((1,), (1,)), ((), ())),
        precision=lax.Precision.HIGHEST, preferred_element_type=f32,
    )
    for d in range(1, R):
        send(eb.at[0], eb.at[d], er_sem, (d,), row_dev(d))

    near = sorted(range(1, R), key=lambda d: -min(d, R - d))

    groups = [(0,)] + [(d, -d) for d in range(1, hy - 1)] + [(hy - 1, 1 - hy, hy)]
    begin = [0] + [2 * g - 1 for g in range(1, len(groups))]

    def give(g):
        for i, d in enumerate(groups[g]):
            rows = jnp.dot(back[...], full[y_of(d)], preferred_element_type=f32).astype(bf16)
            opack[begin[g] + i] = rows.reshape(batches, R, H, BLOCK)
        at = pl.ds(begin[g], len(groups[g]))
        for e in near:
            send(opack.at[at, :, lax.rem(s + e, R)], land.at[at, :, s], ret_sem, (e, g), row_dev(e))
        land[at, :, s] = opack[at, :, s]

    def finish(g):
        at = pl.ds(begin[g], len(groups[g]))
        for e in near:
            arrived(land.at[at, :, lax.rem(s - e + R, R)], ret_sem, (e, g), row_dev(-e))
        for i, d in enumerate(groups[g]):
            rows = pl.ds(pl.multiple_of(y_of(d) * RJ, RJ), RJ)
            for b in range(batches):
                turned = jnp.dot(perm[1], land[begin[g] + i, b].reshape(BLOCK, BLOCK), preferred_element_type=f32)
                turned = turned.reshape(KB, RJ, BLOCK)
                for k in range(KB):
                    out[b * KB + k, rows, :] = (turned[k] * facs[b * KB + k:b * KB + k + 1, :]).astype(bf16)

    def energies(ref, sems, dev, n):
        sum_ = ref[0]
        for d in range(1, n):
            arrived(ref.at[d], sems, (d,), dev(-d))
            sum_ = sum_ + ref[d]
        return sum_

    def energy_row():
        ey[0] = energies(eb, er_sem, row_dev, R)
        for d in range(1, Y):
            send(ey.at[0], ey.at[d], ey_sem, (d,), y_dev(d))

    def factors():
        mean_sq = energies(ey, ey_sem, y_dev, Y) / (fac[...] * (BLOCK * BLOCK))
        fac[...] = lax.rsqrt(mean_sq + epsilon)
        to_smem(fac, fac_s, 3)

        def one(k):
            facs[pl.ds(k, 1), :] = jnp.full((1, BLOCK), fac_s[0, place_of(k) >> 2], f32)

        loop(K, one)

    def ag_come(j):
        hop = 2 if j == hy else 1
        for i in range(PARTS):
            for w in range(2):
                h = i if w == 0 else PARTS - 1 - i
                if j < hy or h in firsts[w]:
                    away = 1 - 2 * w
                    arrived(ag_part(-away * j, h), yag_sem, (w, j - 1, h), y_dev(-away * hop))
                    ag_send(w, j, h)

    last = len(groups) - 1
    forward = pending[:before]
    del pending[:before]
    give(0)
    for j in range(1, last):
        ag_come(j)
        if j == 1:
            energy_row()
        give(j)
    if last == 1:
        energy_row()
    factors()
    sent(forward)
    for g in range(last - 1):
        finish(g)
    ag_come(hy - 1)
    ag_come(hy)
    give(last)
    finish(last - 1)
    for b in range(batches):
        some = xs.at[b, pl.ds(0, 2 * chips - 2)]
        pltpu.make_async_remote_copy(
            src_ref=some, dst_ref=some, send_sem=ya_sem.at[0, b], recv_sem=ya_sem.at[1, b],
            device_id=twin, device_id_type=MESH,
        ).wait_send()
    sent(pending)
    finish(last)


def shards(R, Z, grad_terms, acts, kept, starts):
    Y = lax.axis_size("dp") // R
    tokens, D = grad_terms.shape[1:]
    K = kept.shape[2]
    NB = (acts.shape[1] // BLOCK) * (D // BLOCK)
    rz = BLOCK // Z
    hz, hy = Z // 2, Y // 2
    J = BLOCK // (Y * R)
    H = Y * J
    batches = K // Y
    SR = POOL * Y * R * J
    tab = (-(-(NB // BLOCK + 1) // 8) * 8, BLOCK)
    vmem, smem, dma = pltpu.VMEM, pltpu.SMEM, pltpu.SemaphoreType.DMA
    in_vmem = pl.BlockSpec(memory_space=pltpu.VMEM)
    result = pl.pallas_call(
        functools.partial(body, Y, R, Z, NB),
        out_shape=jax.ShapeDtypeStruct((K, BLOCK, BLOCK), bf16),
        in_specs=[pl.BlockSpec(memory_space=pltpu.HBM)] * 4,
        out_specs=in_vmem,
        scratch_shapes=[
            vmem(acts.shape, bf16),
            vmem(kept.shape[1:], i32),
            smem(kept.shape[1:], i32),
            smem(starts.shape, i32),
            vmem((tokens, D), bf16),
            vmem((2, hz, rz, D), bf16),
            vmem((D // BLOCK, rz, BLOCK), bf16),
            vmem((Z, K, rz, BLOCK), bf16),
            vmem((Z, K, rz, BLOCK), bf16),
            vmem((acts.shape[1] // BLOCK, BLOCK, BLOCK), bf16),
            vmem((2, BLOCK, BLOCK), bf16),
            vmem((Y, Y, R * J, BLOCK), bf16),
            vmem((batches, 2, Y, R // 2, H, BLOCK), bf16),
            vmem((batches, Y, R // 2, 2, H, BLOCK), bf16),
            vmem((batches, Y * R, H, BLOCK), bf16),
            vmem((batches, SR, Y * BLOCK), bf16),
            vmem((SR, BLOCK), f32),
            vmem((BLOCK, BLOCK), f32),
            vmem((R, 8, BLOCK), f32),
            vmem((Y, 8, BLOCK), f32),
            vmem((8, BLOCK), f32),
            vmem((K, BLOCK), f32),
            vmem((Y, SR, BLOCK), bf16),
            vmem((batches * BLOCK, SR), bf16),
            vmem((Y, batches, R, H, BLOCK), bf16),
            vmem((Y, batches, R, H, BLOCK), bf16),
            vmem((8, BLOCK), i32),
            vmem((Z, 8, BLOCK), i32),
            vmem((R,) + tab, i32),
            vmem((Y,) + tab, i32),
            vmem((R, 8, BLOCK), i32),
            vmem((Y, 8, BLOCK), i32),
            vmem(tab, i32),
            vmem((BLOCK, BLOCK), f32),
            smem((Z, 8, BLOCK), i32),
            smem(tab, i32),
            smem(tab, i32),
            smem((8, BLOCK), f32),
            dma((4,)),
            dma((Z,)),
            dma((2, Z)),
            dma((2, R)),
            dma((2, Y)),
            dma((2, R)),
            dma((2, Y)),
            dma((4,)),
            dma((2, 2, hz, SUBS)),
            dma((2, Z, batches)),
            dma((2, batches)),
            dma((2, batches)),
            dma((2, R)),
            dma((2, Y)),
            dma((2, 2, hy, PARTS)),
            dma((2, R, hy)),
        ],
        compiler_params=pltpu.CompilerParams(
            collective_id=0, has_side_effects=True, vmem_limit_bytes=56 * 1024 * 1024
        ),
    )(grad_terms, acts, kept, starts)
    return result[None, None]


def solution(mesh, row=ROW):
    placed = (
        P("tensor", "dp", None),
        P("dp", "tensor"),
        P("dp", "tensor", None),
        P("tensor", None),
    )
    return jax.shard_map(
        functools.partial(shards, row, mesh.shape["tensor"]),
        mesh=mesh,
        in_specs=placed,
        out_specs=P("dp", "tensor", None, None, None),
        check_vma=False,
    )
```

```python
import functools

import jax
import jax.numpy as jnp
from jax import lax
from jax.experimental import pallas as pl
from jax.experimental.pallas import tpu as pltpu
from jax.sharding import PartitionSpec as P

BLOCK = 128
POOL = 4
ROW = 8
SUBS = 4
PARTS = 4
UNROLL = 8

epsilon = 1e-06
MESH = pl.DeviceIdType.MESH
f32, bf16, i32 = jnp.float32, jnp.bfloat16, jnp.int32


def body(
    Y, R, Z, NB,
    grad, acts_in, kept_in, starts_in, out,
    acts, kept, kept_s, starts, own, zr, gsum, pack, gsel, acts_t, perm, tiles, fwd, mid, xs, sel, tot,
    esq, eb, ey, fac, facs, full, back, opack, ostraight, land, mine, kz, mr, my, pr, py, tab, square,
    kz_s, c_s, p_s, fac_s,
    in_sem, own_sem, kz_sem, mr_sem, my_sem, pr_sem, py_sem, loc_sem, zrs_sem, za_sem, xa_sem, ya_sem,
    er_sem, ey_sem, yag_sem, ret_sem, straight_sem,
):
    dp, t = lax.axis_index("dp"), lax.axis_index("tensor")
    y, s = dp // R, lax.rem(dp, R)
    K = out.shape[0]
    D = own.shape[1]
    rz, J = BLOCK // Z, BLOCK // (Y * R)
    cols = D // BLOCK
    KB = Y
    batches = K // KB
    H = KB * J
    RJ = R * J
    owners = Y * R
    SR = POOL * owners * J
    pending = []

    def z_dev(d):
        return (dp, lax.rem(t + d + Z, Z))

    def row_dev(d):
        return (y * R + lax.rem(s + d + R, R), t)

    def y_dev(d):
        return (lax.rem(y + d + Y, Y) * R + s, t)

    chips = Y * R // 2
    chip, core = dp // 2, lax.rem(dp, 2)
    twin = (2 * chip + 1 - core, t)

    def chip_of(i):
        return lax.rem(chip + i, chips)

    def chip_dev(i):
        return (2 * chip_of(i) + core, t)

    def send(src, dst, sems, index, device):
        copy = pltpu.make_async_remote_copy(
            src_ref=src, dst_ref=dst,
            send_sem=sems.at[(0,) + index], recv_sem=sems.at[(1,) + index],
            device_id=device, device_id_type=MESH,
        )
        copy.start()
        pending.append(copy)

    def sent(copies):
        for copy in copies:
            copy.wait_send()

    def arrived(dst, sems, index, device):
        pltpu.make_async_remote_copy(
            src_ref=dst, dst_ref=dst,
            send_sem=sems.at[(0,) + index], recv_sem=sems.at[(1,) + index],
            device_id=device, device_id_type=MESH,
        ).wait_recv()

    def loop(n, step):
        def one(i, _):
            step(i)
            return 0

        lax.fori_loop(0, n, one, 0, unroll=min(UNROLL, n))

    barrier = pltpu.get_barrier_semaphore()
    partners = [z_dev(d) for d in range(1, Z)]
    for device in partners:
        pl.semaphore_signal(barrier, inc=1, device_id=device, device_id_type=MESH)

    def greet(i, _):
        pl.semaphore_signal(barrier, inc=1, device_id=(lax.rem(dp + i, Y * R), t), device_id_type=MESH)
        return 0

    lax.fori_loop(1, Y * R, greet, 0)
    inputs = [
        pltpu.make_async_copy(src, dst, in_sem.at[i])
        for i, (src, dst) in enumerate(((kept_in.at[0], kept), (kept_in.at[0], kept_s), (starts_in, starts), (acts_in, acts)))
    ]
    for copy in inputs:
        copy.start()
    for i in range(Z):
        rows = pl.ds(pl.multiple_of(i * rz, rz), rz)
        pltpu.make_async_copy(grad.at[0, rows, :], own.at[rows, :], own_sem.at[i]).start()
    pl.semaphore_wait(barrier, len(partners) + Y * R - 1)

    hz = Z // 2
    W = D // SUBS
    half = SUBS // 2

    def z_rows(d):
        return pl.ds(pl.multiple_of(lax.rem(t + d + Z, Z) * rz, rz), rz)

    def z_cols(q):
        return pl.ds(q * W, W)

    def z_send(w, j, q, src):
        send(src, zr.at[w, j, :, z_cols(q)], zrs_sem, (w, j, q), z_dev(1 - 2 * w))

    def z_arrived(w, j, q):
        arrived(zr.at[w, j, :, z_cols(q)], zrs_sem, (w, j, q), z_dev(1 - 2 * w))

    firsts = (range(half), range(half, SUBS))
    for i in range(half):
        for w in range(2):
            q = firsts[w][i]
            z_send(w, 0, q, grad.at[0, z_rows((1 - 2 * w) * hz), z_cols(q)])
    if hz > 1:
        for i in range(half):
            for w in range(2):
                q = firsts[1 - w][i]
                z_send(w, 1, q, grad.at[0, z_rows((1 - 2 * w) * (hz - 1)), z_cols(q)])

    for copy in inputs[1:3]:
        copy.wait()
    ids = lax.broadcasted_iota(i32, tab.shape, 0) * BLOCK + lax.broadcasted_iota(i32, tab.shape, 1)

    def mark(k, m):
        return jnp.where(ids == kept_s[0, k], 1, m)

    mr[0] = lax.fori_loop(0, K, mark, jnp.zeros(tab.shape, i32), unroll=min(UNROLL, K))
    for d in range(1, R):
        send(mr.at[0], mr.at[d], mr_sem, (d,), row_dev(d))
    inputs[0].wait()
    mine[...] = jnp.full(mine.shape, -1, i32)
    mine[0:1, 0:K] = kept[...]
    for d in range(1, Z):
        send(mine, kz.at[d], kz_sem, (d,), z_dev(d))
    for i in range(Z):
        rows = pl.ds(pl.multiple_of(i * rz, rz), rz)
        pltpu.make_async_copy(grad.at[0, rows, :], own.at[rows, :], own_sem.at[i]).wait()

    def to_smem(src, dst, i):
        copy = pltpu.make_async_copy(src, dst, loc_sem.at[i])
        copy.start()
        copy.wait()

    def gathered(ref, sems, dev, n):
        for d in range(1, n):
            arrived(ref.at[d], sems, (d,), dev(-d))
        m = ref[0]
        for d in range(1, n):
            m = jnp.maximum(m, ref[d])
        return m

    def marks_row():
        my[0] = gathered(mr, mr_sem, row_dev, R)
        for d in range(1, Y):
            send(my.at[0], my.at[d], my_sem, (d,), y_dev(d))

    def ranks():
        kz[0] = mine[...]
        for d in range(1, Z):
            arrived(kz.at[d], kz_sem, (d,), z_dev(-d))
        to_smem(kz, kz_s, 0)

    def places():
        m = gathered(my, my_sem, y_dev, Y)
        lane = lax.broadcasted_iota(i32, tab.shape, 1)
        sub = lax.broadcasted_iota(i32, tab.shape, 0)
        run = m
        step = 1
        while step < BLOCK:
            run = run + jnp.where(lane >= step, pltpu.roll(run, step, 1), 0)
            step *= 2
        total = jnp.broadcast_to(run[:, BLOCK - 1:BLOCK], tab.shape)
        above = total
        step = 1
        while step < tab.shape[0]:
            above = above + jnp.where(sub >= step, pltpu.roll(above, step, 0), 0)
            step *= 2
        count = run + above - total - m
        tab[...] = count
        to_smem(tab, c_s, 1)

        def region(o, carry):
            base, before = carry
            first = starts[0, o]
            inside = ids >= first
            there = c_s[first >> 7, first & 127]
            return jnp.where(inside, o * POOL, base), jnp.where(inside, there, before)

        zero = jnp.zeros(tab.shape, i32)
        base, before = lax.fori_loop(0, owners, region, (zero, zero), unroll=UNROLL)
        tab[...] = base + count - before
        to_smem(tab, p_s, 2)

        sub8 = lax.broadcasted_iota(i32, (8, BLOCK), 0)
        lane8 = lax.broadcasted_iota(i32, (8, BLOCK), 1)

        def fill(k, tile):
            here = (sub8 == lax.div(k, KB)) & (lax.div(lane8, J) == s * KB + lax.rem(k, KB))
            return jnp.where(here, place_of(k) * J + lax.rem(lane8, J), tile)

        pr[0] = lax.fori_loop(0, K, fill, jnp.full((8, BLOCK), -1, i32), unroll=min(UNROLL, K))
        for d in range(1, R):
            send(pr.at[0], pr.at[d], pr_sem, (d,), row_dev(d))

    def place_of(k):
        block = kept_s[0, k]
        return p_s[block >> 7, block & 127]

    def places_row():
        py[y] = gathered(pr, pr_sem, row_dev, R)
        for d in range(1, Y):
            send(py.at[y], py.at[y], py_sem, (d,), y_dev(d))

    half0 = range(batches // 2)
    halves = (half0, range(len(half0), batches))
    ways = [(0, range(batches)), (1, range(batches)), (2, halves[0]), (-1, range(batches)), (-2, halves[1])]

    def going_back():
        lane = lax.broadcasted_iota(i32, (BLOCK, SR), 1).astype(f32)
        square[...] = jnp.zeros(square.shape, f32)
        for i, (away, parts) in enumerate(ways):
            square[0:8, :] = py[lax.rem(y + away + Y, Y)].astype(f32)
            turned = square[...].T
            for b in parts:
                rows = jnp.where(turned[:, b:b + 1] == lane, 1.0, 0.0).astype(bf16)
                back[i, b * BLOCK:(b + 1) * BLOCK, :] = rows

    def places_all():
        for d in range(1, Y):
            arrived(py.at[lax.rem(y - d + Y, Y)], py_sem, (d,), y_dev(-d))

    def select(b):
        row = lax.broadcasted_iota(i32, (SR, BLOCK), 0)

        def one(i, _):
            at = pl.ds(pl.multiple_of(i * BLOCK, BLOCK), BLOCK)
            sel[b, :, at] = jnp.where(py[i][b:b + 1, :] == row, 1.0, 0.0).astype(bf16)
            return 0

        lax.fori_loop(0, Y, one, 0)

    def counts():
        lane = lax.broadcasted_iota(i32, (8, BLOCK), 1)

        def one(o, n):
            first = starts[0, o]
            after = starts[0, jnp.minimum(o + 1, owners - 1)]
            after = jnp.where(o + 1 < owners, after, NB)
            there = c_s[after >> 7, after & 127] - c_s[first >> 7, first & 127]
            return jnp.where(lane == o, there, n)

        n = lax.fori_loop(0, owners, one, jnp.ones((8, BLOCK), i32), unroll=UNROLL)
        fac[...] = jnp.maximum(n, 1).astype(f32)

    order = (tuple(firsts[1]) + tuple(firsts[0]), tuple(firsts[0]) + tuple(firsts[1]))
    CH = min(512, W)

    def z_add(w, j, q, d):
        rows = z_rows(d)

        def add(c):
            at = pl.ds(pl.multiple_of(q * W + c * CH, CH), CH)
            zr[w, j, :, at] = (zr[w, j, :, at].astype(f32) + own[rows, at].astype(f32)).astype(bf16)

        loop(W // CH, add)

    chores = {(1, SUBS - 1): marks_row, (2, 1): ranks, (2, SUBS - 1): places, (3, SUBS - 1): places_row}
    for j in range(1, hz):
        for i in range(SUBS):
            for w in range(2):
                q = order[w][i]
                if j == 1 and q not in firsts[w]:
                    continue
                z_arrived(w, j - 1, q)
                z_add(w, j - 1, q, (1 - 2 * w) * (hz - j))
                z_send(w, j, q, zr.at[w, j - 1, :, z_cols(q)])
            if (j, i) in chores:
                chores.pop((j, i))()
    for chore in chores.values():
        chore()
    mine_rows = z_rows(0)
    for q in [q for pair in zip(*firsts) for q in pair]:
        for w in range(2):
            if hz > 1 or q in firsts[w]:
                z_arrived(w, hz - 1, q)

        def total_cols(c):
            at = pl.ds(pl.multiple_of(q * W + c * CH, CH), CH)
            sum_ = own[mine_rows, at].astype(f32)
            for w in range(2):
                if hz > 1 or q in firsts[w]:
                    sum_ = sum_ + zr[w, hz - 1, :, at].astype(f32)
            for i in range(CH // BLOCK):
                gsum[q * (W // BLOCK) + c * (CH // BLOCK) + i] = sum_[:, i * BLOCK:(i + 1) * BLOCK].astype(bf16)

        loop(W // CH, total_cols)

    far = sorted(range(1, Z), key=lambda d: -min(d, Z - d))

    def set_up():
        inputs[3].wait()
        for i in range(acts.shape[1] // BLOCK):
            block = acts[:, i * BLOCK:(i + 1) * BLOCK].astype(f32)
            acts_t[i] = block.T.astype(bf16)
        to = lax.broadcasted_iota(i32, (BLOCK, BLOCK), 0)
        frm = lax.broadcasted_iota(i32, (BLOCK, BLOCK), 1)
        for i, (outer, inner) in enumerate(((R, KB), (KB, R))):
            a, b, c = lax.div(to, inner * J), lax.rem(lax.div(to, J), inner), lax.rem(to, J)
            perm[i] = jnp.where(frm == (b * outer + a) * J + c, 1.0, 0.0).astype(bf16)

    def selects():
        places_all()
        for b in range(batches):
            select(b)
        counts()

    early = pending[:]
    pending.clear()
    chores = [set_up, selects, going_back, functools.partial(sent, early)]
    for b in range(batches):
        batch = pl.ds(b * KB, KB)
        for d in far:
            def put(i):
                col = lax.rem(kz_s[(Z - d) % Z, 0, b * KB + i], cols)
                pack[d, b * KB + i] = gsum[col]

            loop(KB, put)
            send(pack.at[d, batch], gsel.at[t, batch], za_sem, (d, b), z_dev(d))

        def keep(i):
            col = lax.rem(kz_s[0, 0, b * KB + i], cols)
            gsel[t, b * KB + i] = gsum[col]

        loop(KB, keep)
        if chores:
            chores.pop(0)()
    for chore in chores:
        chore()

    for b in range(batches):
        batch = pl.ds(b * KB, KB)
        for d in far:
            arrived(gsel.at[lax.rem(t - d + Z, Z), batch], za_sem, (d, b), z_dev(-d))
        for i in range(KB):
            k = b * KB + i
            left = acts_t[lax.div(kept_s[0, k], cols)]
            right = gsel[:, k].reshape(BLOCK, BLOCK)
            product = jnp.dot(left, right, preferred_element_type=f32).astype(bf16)
            tiles[:, i] = product.reshape(Y, RJ, BLOCK)
        for i in range(Y):
            turned = jnp.dot(perm[0], tiles[i].reshape(BLOCK, BLOCK), preferred_element_type=f32)
            turned = turned.astype(bf16).reshape(R // 2, 2, H, BLOCK)
            for c in range(2):
                fwd[b, c, i] = turned[:, c]
        send(fwd.at[b, 1 - core], mid.at[b, :, :, core], xa_sem, (b,), twin)
        mid[b, :, :, core] = fwd[b, core]
        arrived(mid.at[b, :, :, 1 - core], xa_sem, (b,), twin)

        def direct(i, _):
            to = chip_of(i)
            pltpu.make_async_remote_copy(
                src_ref=mid.at[b, to // (R // 2), lax.rem(to, R // 2)], dst_ref=xs.at[b, pl.ds(2 * chip, 2)],
                send_sem=ya_sem.at[0, b], recv_sem=ya_sem.at[1, b],
                device_id=chip_dev(i), device_id_type=MESH,
            ).start()
            return 0

        lax.fori_loop(1, chips, direct, 0)
        pltpu.make_async_copy(
            mid.at[b, y, s // 2], xs.at[b, pl.ds(2 * chip, 2)], ya_sem.at[1, b]
        ).start()

    for b in range(batches):
        arrived(xs.at[b], ya_sem, (b,), twin)
        here = jnp.dot(sel[b], xs[b].reshape(Y * BLOCK, BLOCK), preferred_element_type=f32)
        tot[...] = here if b == 0 else tot[...] + here

    hy = Y // 2
    HS = SR // PARTS
    firsts = (range(PARTS // 2), range(PARTS // 2, PARTS))

    def y_of(d):
        return lax.rem(y + d + Y, Y)

    def ag_part(d, h):
        return full.at[y_of(d), pl.ds(h * HS, HS)]

    def ag_send(w, j, h):
        if j < hy - 2:
            away = 1 - 2 * w
            send(ag_part(-away * j, h), ag_part(-away * j, h), yag_sem, (w, j, h), y_dev(away))

    before = len(pending)
    full[y] = tot[...].astype(bf16)
    for i in range(PARTS):
        for w in range(2):
            ag_send(w, 0, (i if w == 0 else PARTS - 1 - i))
    squares = jnp.sum((tot[...] * tot[...]).reshape(owners, POOL * J, BLOCK), axis=1)
    esq[...] = jnp.zeros(esq.shape, f32)
    esq[0:owners, :] = squares
    eb[0] = lax.dot_general(
        jnp.ones((8, BLOCK), f32), esq[...], (((1,), (1,)), ((), ())),
        precision=lax.Precision.HIGHEST, preferred_element_type=f32,
    )
    for d in range(1, R):
        send(eb.at[0], eb.at[d], er_sem, (d,), row_dev(d))

    near = sorted(range(1, R), key=lambda d: -min(d, R - d))

    groups = [(0,)] + [(d, -d) for d in range(1, hy - 1)] + [(hy - 1, 1 - hy, hy)]
    begin = [0] + [2 * g - 1 for g in range(1, len(groups))]
    last = len(groups) - 1

    def give(g):
        for i, d in enumerate(groups[g]):
            rows = jnp.dot(back[0], full[y_of(d)], preferred_element_type=f32).astype(bf16)
            opack[begin[g] + i] = rows.reshape(batches, R, H, BLOCK)
        at = pl.ds(begin[g], len(groups[g]))
        for e in near:
            send(opack.at[at, :, lax.rem(s + e, R)], land.at[at, :, s], ret_sem, (e, g), row_dev(e))
        land[at, :, s] = opack[at, :, s]

    def way(w, hop):
        i = 2 * w + hop
        parts = ways[i][1]
        return i, hop * (1 - 2 * w), pl.ds(parts[0], len(parts)), begin[last] + (2 if hop == 2 else 1 - w)

    both = [(w, hop) for hop in (1, 2) for w in range(2) if len(ways[2 * w + hop][1])]

    def straight():
        for w, hop in both:
            i, away, parts, at = way(w, hop)
            chunk = full[y_of(-(1 - 2 * w) * (hy - 2))]
            rows = jnp.dot(
                back[i, pl.ds(parts.start * BLOCK, parts.size * BLOCK), :], chunk, preferred_element_type=f32
            )
            ostraight[i - 1, parts] = rows.astype(bf16).reshape(parts.size, R, H, BLOCK)
            for e in range(R):
                to = lax.rem(s + e, R)
                send(
                    ostraight.at[i - 1, parts, to], land.at[at, parts, s], straight_sem, (i - 1, e),
                    (y_of(away) * R + to, t),
                )

    def place_rows(at, d):
        rows = pl.ds(pl.multiple_of(y_of(d) * RJ, RJ), RJ)
        for b in range(batches):
            turned = jnp.dot(perm[1], land[at, b].reshape(BLOCK, BLOCK), preferred_element_type=f32)
            turned = turned.reshape(KB, RJ, BLOCK)
            for k in range(KB):
                out[b * KB + k, rows, :] = (turned[k] * facs[b * KB + k:b * KB + k + 1, :]).astype(bf16)

    def finish(g):
        at = pl.ds(begin[g], len(groups[g]))
        for e in near:
            arrived(land.at[at, :, lax.rem(s - e + R, R)], ret_sem, (e, g), row_dev(-e))
        for i, d in enumerate(groups[g]):
            place_rows(begin[g] + i, d)

    def finish_straight():
        for w, hop in both:
            i, away, parts, at = way(w, hop)
            for e in range(R):
                come = lax.rem(s - e + R, R)
                arrived(land.at[at, parts, come], straight_sem, (i - 1, e), (y_of(-away) * R + come, t))
            if hop == 1:
                place_rows(at, groups[last][1 - w])
        place_rows(begin[last] + 2, hy)

    def energies(ref, sems, dev, n):
        sum_ = ref[0]
        for d in range(1, n):
            arrived(ref.at[d], sems, (d,), dev(-d))
            sum_ = sum_ + ref[d]
        return sum_

    def energy_row():
        ey[0] = energies(eb, er_sem, row_dev, R)
        for d in range(1, Y):
            send(ey.at[0], ey.at[d], ey_sem, (d,), y_dev(d))

    def factors():
        mean_sq = energies(ey, ey_sem, y_dev, Y) / (fac[...] * (BLOCK * BLOCK))
        fac[...] = lax.rsqrt(mean_sq + epsilon)
        to_smem(fac, fac_s, 3)

        def one(k):
            facs[pl.ds(k, 1), :] = jnp.full((1, BLOCK), fac_s[0, place_of(k) >> 2], f32)

        loop(K, one)

    def ag_come(j):
        for i in range(PARTS):
            for w in range(2):
                h = i if w == 0 else PARTS - 1 - i
                away = 1 - 2 * w
                arrived(ag_part(-away * j, h), yag_sem, (w, j - 1, h), y_dev(-away))
                ag_send(w, j, h)

    forward = pending[:before]
    del pending[:before]
    give(0)
    for j in range(1, last):
        ag_come(j)
        if j == 1:
            energy_row()
        if j == last - 1:
            straight()
        give(j)
    if last == 1:
        straight()
        energy_row()
    factors()
    sent(forward)
    for g in range(last):
        finish(g)
    for b in range(batches):
        some = xs.at[b, pl.ds(0, 2 * chips - 2)]
        pltpu.make_async_remote_copy(
            src_ref=some, dst_ref=some, send_sem=ya_sem.at[0, b], recv_sem=ya_sem.at[1, b],
            device_id=twin, device_id_type=MESH,
        ).wait_send()
    sent(pending)
    finish_straight()


def shards(R, Z, grad_terms, acts, kept, starts):
    Y = lax.axis_size("dp") // R
    tokens, D = grad_terms.shape[1:]
    K = kept.shape[2]
    NB = (acts.shape[1] // BLOCK) * (D // BLOCK)
    rz = BLOCK // Z
    hz, hy = Z // 2, Y // 2
    J = BLOCK // (Y * R)
    H = Y * J
    batches = K // Y
    SR = POOL * Y * R * J
    tab = (-(-(NB // BLOCK + 1) // 8) * 8, BLOCK)
    vmem, smem, dma = pltpu.VMEM, pltpu.SMEM, pltpu.SemaphoreType.DMA
    in_vmem = pl.BlockSpec(memory_space=pltpu.VMEM)
    result = pl.pallas_call(
        functools.partial(body, Y, R, Z, NB),
        out_shape=jax.ShapeDtypeStruct((K, BLOCK, BLOCK), bf16),
        in_specs=[pl.BlockSpec(memory_space=pltpu.HBM)] * 4,
        out_specs=in_vmem,
        scratch_shapes=[
            vmem(acts.shape, bf16),
            vmem(kept.shape[1:], i32),
            smem(kept.shape[1:], i32),
            smem(starts.shape, i32),
            vmem((tokens, D), bf16),
            vmem((2, hz, rz, D), bf16),
            vmem((D // BLOCK, rz, BLOCK), bf16),
            vmem((Z, K, rz, BLOCK), bf16),
            vmem((Z, K, rz, BLOCK), bf16),
            vmem((acts.shape[1] // BLOCK, BLOCK, BLOCK), bf16),
            vmem((2, BLOCK, BLOCK), bf16),
            vmem((Y, Y, R * J, BLOCK), bf16),
            vmem((batches, 2, Y, R // 2, H, BLOCK), bf16),
            vmem((batches, Y, R // 2, 2, H, BLOCK), bf16),
            vmem((batches, Y * R, H, BLOCK), bf16),
            vmem((batches, SR, Y * BLOCK), bf16),
            vmem((SR, BLOCK), f32),
            vmem((BLOCK, BLOCK), f32),
            vmem((R, 8, BLOCK), f32),
            vmem((Y, 8, BLOCK), f32),
            vmem((8, BLOCK), f32),
            vmem((K, BLOCK), f32),
            vmem((Y, SR, BLOCK), bf16),
            vmem((5, batches * BLOCK, SR), bf16),
            vmem((Y, batches, R, H, BLOCK), bf16),
            vmem((4, batches, R, H, BLOCK), bf16),
            vmem((Y, batches, R, H, BLOCK), bf16),
            vmem((8, BLOCK), i32),
            vmem((Z, 8, BLOCK), i32),
            vmem((R,) + tab, i32),
            vmem((Y,) + tab, i32),
            vmem((R, 8, BLOCK), i32),
            vmem((Y, 8, BLOCK), i32),
            vmem(tab, i32),
            vmem((BLOCK, BLOCK), f32),
            smem((Z, 8, BLOCK), i32),
            smem(tab, i32),
            smem(tab, i32),
            smem((8, BLOCK), f32),
            dma((4,)),
            dma((Z,)),
            dma((2, Z)),
            dma((2, R)),
            dma((2, Y)),
            dma((2, R)),
            dma((2, Y)),
            dma((4,)),
            dma((2, 2, hz, SUBS)),
            dma((2, Z, batches)),
            dma((2, batches)),
            dma((2, batches)),
            dma((2, R)),
            dma((2, Y)),
            dma((2, 2, hy, PARTS)),
            dma((2, R, hy)),
            dma((2, 4, R)),
        ],
        compiler_params=pltpu.CompilerParams(
            collective_id=0, has_side_effects=True, vmem_limit_bytes=56 * 1024 * 1024
        ),
    )(grad_terms, acts, kept, starts)
    return result[None, None]


def solution(mesh, row=ROW):
    placed = (
        P("tensor", "dp", None),
        P("dp", "tensor"),
        P("dp", "tensor", None),
        P("tensor", None),
    )
    return jax.shard_map(
        functools.partial(shards, row, mesh.shape["tensor"]),
        mesh=mesh,
        in_specs=placed,
        out_specs=P("dp", "tensor", None, None, None),
        check_vma=False,
    )
```
